1024 devices in a mesh: dom: 128 (over x, y, core), col: 8 (over z).
Axes of the slice: x: 8, y: 8, z: 8, core: 2. Of those that a mesh axis runs over, the one named last changes fastest.
Arguments:
- states: bfloat16 [256, 131072], P('col', 'dom'), may hold values from -6 to 6
- diag_blocks: bfloat16 [131072, 1024], P('dom'), may hold values from -0.1875 to 0.1875
- coupling: bfloat16 [131072, 1024], P('dom'), may hold values from -0.1875 to 0.1875
- counts: int32 [128], P('dom'), may hold values from 512 to 1024, as said below
Outputs:
- basis: float32 [256, 131072], P('col', 'dom')
- reduced: float32 [256, 256], replicated
The draws below stay inside these ranges and needn't reach their ends.
Inputs may be any that keep to these rules, and one draw needn't show every extreme that they name: `counts`: each domain uses between 512 and 1024 slots; one domain uses all 1024.
All inputs are finite; a program needn't handle non-finite values.
Results may differ from the reference program's by a relative error of at most 0.0046.
Values may be sent and summed in bfloat16 or wider, within the bound.
No kernel may reach another device: no remote copies, remote signals or barrier semaphores. Data moves between devices by JAX's collectives and lax.ppermute only.
A program may use at most 32 MiB of HBM per device.

```python
import math
import jax
import jax.numpy as jnp
from jax import lax

NSTATE = 256
ROWS = 1024
DEGREE = 3
DOMAINS = 128
ORBITALS = 131072


def draw_counts(key, part):
    key = jax.random.fold_in(key, 11)
    key_base, key_full = jax.random.split(key)
    base = jax.random.randint(key_base, (DOMAINS,), ROWS // 2, ROWS + 1)
    full = jax.random.randint(key_full, (), 0, DOMAINS)
    return jnp.where(jnp.arange(DOMAINS) == full, ROWS, base).astype(jnp.int32)


def block_scale(key, extent, cuts, least, top_value):
    def one(dim, blocks):
        heights = jax.random.uniform(jax.random.fold_in(jax.random.fold_in(key, 6), dim), (blocks,), jnp.float32, least / len(cuts), top_value / len(cuts))
        return jnp.repeat(jnp.exp(heights), extent[dim] // blocks).reshape((-1,) + (1,) * (len(extent) - dim - 1))

    gain = one(*cuts[0])
    for cut in cuts[1:]:
        gain = gain * one(*cut)
    return gain


def gaussian(own_key, shape, deviation, bound, pieces=(), held_as=jnp.bfloat16):
    entries = jax.random.normal(own_key, shape, jnp.float32) * deviation
    if len(pieces) > 0:
        entries = block_scale(own_key, shape, pieces, -0.22, 0.18) * entries
    return jnp.clip(entries, min=-bound, max=bound).astype(held_as)


def setup_inputs(seed: int = 0) -> dict:
    splits = jax.random.split(jax.random.key(seed), 5)
    states = gaussian(splits[0], (NSTATE, ORBITALS), 1.0, 6.0, ((0, 8), (1, 128)))
    diag_blocks = gaussian(splits[1], (ORBITALS, ROWS), ROWS ** -0.5, 0.1875, ((0, 128),))
    coupling = gaussian(splits[2], (ORBITALS, ROWS), ROWS ** -0.5, 0.1875, ((0, 128),))
    counts = draw_counts(jax.random.fold_in(splits[4], 71), 0)
    return dict(states=states, diag_blocks=diag_blocks, coupling=coupling, counts=counts)


HIGH = lax.Precision.HIGHEST
CENTER = 0.5
HALF = 2.0

def apply_op(block, diag_all, coup_all, live):
    fblock = block.astype(jnp.float32)
    own = jnp.einsum('sdr,drq->sdq', fblock, diag_all, precision=HIGH)
    own_t = jnp.einsum('sdr,dqr->sdq', fblock, diag_all, precision=HIGH)
    onward = jnp.einsum('sdr,drq->sdq', fblock, coup_all, precision=HIGH)
    zeros = jnp.zeros_like(onward[:, :1])
    from_prev = jnp.concatenate([zeros, onward[:, :-1]], axis=1)
    next_block = jnp.concatenate([fblock[:, 1:], jnp.zeros_like(fblock[:, :1])], axis=1)
    from_next = jnp.einsum('sdr,dqr->sdq', next_block, coup_all, precision=HIGH)
    return live * (0.5 * (own + own_t) + from_prev + from_next)

def reference(states, diag_blocks, coupling, counts):
    diag_all = diag_blocks.astype(jnp.float32).reshape(DOMAINS, ROWS, ROWS)
    coup_all = coupling.astype(jnp.float32).reshape(DOMAINS, ROWS, ROWS)
    slots = jnp.arange(ROWS, dtype=jnp.int32)
    live = (slots[None, :] < counts[:, None]).astype(jnp.float32)[None, :, :]
    first = live * states.astype(jnp.float32).reshape(NSTATE, DOMAINS, ROWS)
    prev = first
    cur = (apply_op(first.astype(jnp.bfloat16), diag_all, coup_all, live) - CENTER * first) / HALF
    for step in range(DEGREE - 1):
        nxt = 2.0 * (apply_op(cur.astype(jnp.bfloat16), diag_all, coup_all, live) - CENTER * cur) / HALF - prev
        prev = cur
        cur = nxt
    filtered = cur.astype(jnp.bfloat16)
    image = apply_op(filtered, diag_all, coup_all, live).astype(jnp.bfloat16)
    flat = filtered.reshape(NSTATE, DOMAINS * ROWS)
    flat_image = image.reshape(NSTATE, DOMAINS * ROWS)
    gram = jnp.dot(flat.astype(jnp.float32), flat.T.astype(jnp.float32), preferred_element_type=jnp.float32)
    proj = jnp.dot(flat.astype(jnp.float32), flat_image.T.astype(jnp.float32), preferred_element_type=jnp.float32)
    lower = jnp.linalg.cholesky(gram)
    inverse = lax.linalg.triangular_solve(lower, jnp.eye(NSTATE, dtype=jnp.float32), left_side=True, lower=True)
    reduced = jnp.dot(jnp.dot(inverse, proj, precision=HIGH), inverse.T, precision=HIGH)
    basis = math.sqrt(DOMAINS * ROWS) * jnp.dot(inverse, flat.astype(jnp.float32), precision=HIGH)
    return (basis, reduced)
```

```python
import math

import jax
import jax.numpy as jnp
from jax import lax
from jax.experimental import pallas as pl
from jax.experimental.pallas import tpu as pltpu
from jax.sharding import Mesh
from jax.sharding import PartitionSpec as P

DEGREE = 3
HIGH = lax.Precision.HIGHEST
CENTER = 0.5
HALF = 2.0
TRANSPOSED = (((1,), (1,)), ((), ()))
FIRST_WITH_FIRST = (((0,), (0,)), ((), ()))
ALONG_X, ALONG_Y, CORES = 8, 8, 2
DOM = ("x", "y", "core")
WIDE = 64
F32 = jnp.float32
BF16 = jnp.bfloat16


def factor_rows(block, wide):
    done = []
    rest = block
    for start in range(0, wide, 8):
        cols = [
            jnp.broadcast_to(rest[:, start + q : start + q + 1], rest.shape) for q in range(8)
        ]
        rows = [rest[q : q + 1, :] for q in range(8)]
        scaled = []
        for p in range(8):
            pivot = cols[p][p : p + 1, :]
            inv = 1.0 / pivot
            scaled.append(rows[p] * inv)
            for q in range(p + 1, 8):
                link = cols[p][q : q + 1, :]
                rows[q] = rows[q] - link * scaled[p]
                cols[q] = cols[q] - cols[p] * (link * inv)
            done.append(rows[p] * lax.rsqrt(pivot))
        if start + 8 < wide:
            change = cols[0][8:, :] * scaled[0]
            for p in range(1, 8):
                change = change + cols[p][8:, :] * scaled[p]
            rest = rest[8:, :] - change
    return jnp.concatenate(done, axis=0)


def cholesky_inverse(a_ref, x_ref, inv_ref):
    n, w = a_ref.shape[0], WIDE
    i = lax.broadcasted_iota(jnp.int32, (n, n), 0)
    j = lax.broadcasted_iota(jnp.int32, (n, n), 1)
    x_ref[...] = (i == j).astype(F32)
    eye = x_ref[:w, :w]
    for s in range(0, n, w):
        here = slice(s, s + w)
        block = factor_rows(jnp.concatenate([a_ref[here, here], eye], axis=1), w)
        both = jnp.concatenate([a_ref[here, :], x_ref[here, :]], axis=1)
        out = jnp.dot(block[:, w:], both, precision=HIGH, preferred_element_type=F32)
        inv_ref[here, :] = out[:, n:]
        if s + w < n:
            change = lax.dot_general(
                out[:, s + w : n], out, FIRST_WITH_FIRST, precision=HIGH, preferred_element_type=F32
            )
            a_ref[s + w :, :] = a_ref[s + w :, :] - change[:, :n]
            x_ref[s + w :, :] = x_ref[s + w :, :] - change[:, n:]


def finish_kernel(col_ref, sums_ref, all_ref, basis_ref, reduced_ref, a_ref, q_ref, x_ref, inv_ref):
    tiles, cols, eight, lanes = sums_ref.shape
    local = basis_ref.shape[0]
    per_matrix = tiles // 2
    halves = a_ref.shape[1] // lanes
    for t in range(tiles):
        target = a_ref if t < per_matrix else q_ref
        block, half = divmod(t % per_matrix, halves)
        for z in range(cols):
            top = z * local + block * eight
            target[top : top + eight, half * lanes : (half + 1) * lanes] = sums_ref[t, z]
    cholesky_inverse(a_ref, x_ref, inv_ref)
    proj = q_ref[...]
    proj = 0.5 * (proj + proj.T)
    inverse = inv_ref[...]
    left = jnp.dot(inverse, proj, precision=HIGH, preferred_element_type=F32)
    reduced_ref[...] = lax.dot_general(
        left, inverse, TRANSPOSED, precision=HIGH, preferred_element_type=F32
    )
    scale = math.sqrt(ALONG_X * ALONG_Y * CORES * basis_ref.shape[1])
    mine = scale * inv_ref[pl.ds(pl.multiple_of(col_ref[0] * local, local), local), :]
    high = mine.astype(BF16)
    low = (mine - high.astype(F32)).astype(BF16)
    states = all_ref[...]
    basis_ref[...] = jnp.dot(high, states, preferred_element_type=F32) + jnp.dot(
        low, states, preferred_element_type=F32
    )


def finish(col, sums, all_states, local):
    total, rows = all_states.shape
    vmem = pl.BlockSpec(memory_space=pltpu.VMEM)
    square = pltpu.VMEM((total, total), F32)
    return pl.pallas_call(
        finish_kernel,
        out_shape=(
            jax.ShapeDtypeStruct((local, rows), F32),
            jax.ShapeDtypeStruct((total, total), F32),
        ),
        in_specs=[pl.BlockSpec(memory_space=pltpu.SMEM), vmem, vmem],
        out_specs=(vmem, vmem),
        scratch_shapes=[square] * 4,
        compiler_params=pltpu.CompilerParams(vmem_limit_bytes=32 * 2**20),
        cost_estimate=pl.CostEstimate(flops=2 * 10**8, bytes_accessed=2**21, transcendentals=0),
    )(col, sums, all_states)


def across_pairs(count):
    pairs = [(i, i + 1 if i % 2 else i - 1) for i in range(count)]
    return [(i, j) for i, j in pairs if 0 <= j < count]


def body(states, diag_blocks, coupling, counts):
    rows = diag_blocks.shape[1]
    local = states.shape[0]
    domains = lax.axis_size(DOM)
    live = (lax.iota(jnp.int32, rows) < counts[0]).astype(F32)[None, :]
    even = lax.axis_index("core") == 0

    def trade(block, onward):
        over = lax.ppermute(jnp.where(even, block, onward), DOM, across_pairs(domains))
        both = lax.all_gather(jnp.where(even, onward, block), "core")
        beside = jnp.where(even, both[1], both[0])
        return jnp.where(even, over, beside), jnp.where(even, beside, over)

    def apply_op(block):
        low = block.astype(BF16)
        onward = jnp.dot(low, coupling, preferred_element_type=F32)
        from_prev, next_block = trade(block, onward)
        own = jnp.dot(low, diag_blocks, preferred_element_type=F32)
        own_t = lax.dot_general(low, diag_blocks, TRANSPOSED, preferred_element_type=F32)
        from_next = lax.dot_general(
            next_block.astype(BF16), coupling, TRANSPOSED, preferred_element_type=F32
        )
        return live * (0.5 * (own + own_t) + from_prev + from_next)

    first = live * states.astype(F32)
    prev = first
    cur = (apply_op(first) - CENTER * first) / HALF
    for step in range(DEGREE - 1):
        prev, cur = cur, 2.0 * (apply_op(cur) - CENTER * cur) / HALF - prev
    filtered = cur.astype(BF16)

    onward = jnp.dot(filtered, coupling, preferred_element_type=F32).astype(BF16)
    arrived = lax.ppermute(onward, DOM, [(i, i + 1) for i in range(domains - 1)])
    cols = lax.axis_size("col")
    all_states = lax.all_to_all(
        jnp.broadcast_to(filtered[None], (cols, local, rows)), "col", 0, 0
    ).reshape(cols * local, rows)
    half_image = jnp.dot(filtered, diag_blocks, preferred_element_type=F32)
    half_image = (half_image + 2.0 * arrived.astype(F32)).astype(BF16)

    total = cols * local
    pair = jnp.concatenate([filtered, half_image], axis=0)
    terms = lax.dot_general(pair, all_states, TRANSPOSED, preferred_element_type=F32)
    peers = ALONG_Y * CORES
    tiles = terms.reshape(2 * local // 8, 8, total // 128, 128)
    tiles = tiles.transpose(0, 2, 1, 3).reshape(peers, -1, 8, 128)
    share = lax.all_to_all(tiles, ("y", "core"), 0, 0).sum(0)
    shares = jnp.broadcast_to(share[None], (ALONG_X * cols,) + share.shape)
    shares = lax.all_to_all(shares, ("x", "col"), 0, 0)
    share = shares.reshape((ALONG_X, cols) + share.shape).sum(0)
    spread = jnp.broadcast_to(share[None], (peers,) + share.shape)
    sums = lax.all_to_all(spread, ("y", "core"), 0, 0)
    sums = sums.reshape(peers, cols, 8, 128)
    col = lax.axis_index("col").astype(jnp.int32).reshape(1)
    return finish(col, sums, all_states, local)


def solution(mesh):
    shape = (ALONG_X, ALONG_Y, CORES, mesh.shape["col"])
    fine = Mesh(mesh.devices.reshape(shape), DOM + ("col",))
    placed = (P("col", DOM), P(DOM, None), P(DOM, None), P(DOM))
    return jax.shard_map(
        body, mesh=fine, in_specs=placed, out_specs=(P("col", DOM), P()), check_vma=False
    )
```

```python
import math

import jax
import jax.numpy as jnp
from jax import lax
from jax.experimental import pallas as pl
from jax.experimental.pallas import tpu as pltpu
from jax.sharding import Mesh
from jax.sharding import PartitionSpec as P

DEGREE = 3
HIGH = lax.Precision.HIGHEST
CENTER = 0.5
HALF = 2.0
TRANSPOSED = (((1,), (1,)), ((), ()))
FIRST_WITH_FIRST = (((0,), (0,)), ((), ()))
ALONG_X, ALONG_Y, CORES = 8, 8, 2
DOM = ("x", "y", "core")
WIDE = 64
F32 = jnp.float32
BF16 = jnp.bfloat16


def factor_rows(block, wide):
    done = []
    rest = block
    for start in range(0, wide, 8):
        cols = [
            jnp.broadcast_to(rest[:, start + q : start + q + 1], rest.shape) for q in range(8)
        ]
        rows = [rest[q : q + 1, :] for q in range(8)]
        scaled = []
        for p in range(8):
            pivot = cols[p][p : p + 1, :]
            inv = 1.0 / pivot
            scaled.append(rows[p] * inv)
            for q in range(p + 1, 8):
                link = cols[p][q : q + 1, :]
                rows[q] = rows[q] - link * scaled[p]
                cols[q] = cols[q] - cols[p] * (link * inv)
            done.append(rows[p] * lax.rsqrt(pivot))
        if start + 8 < wide:
            change = cols[0][8:, :] * scaled[0]
            for p in range(1, 8):
                change = change + cols[p][8:, :] * scaled[p]
            rest = rest[8:, :] - change
    return jnp.concatenate(done, axis=0)


def cholesky_inverse(a_ref, x_ref, inv_ref):
    n, w = a_ref.shape[0], WIDE
    i = lax.broadcasted_iota(jnp.int32, (n, n), 0)
    j = lax.broadcasted_iota(jnp.int32, (n, n), 1)
    x_ref[...] = (i == j).astype(F32)
    eye = x_ref[:w, :w]
    for s in range(0, n, w):
        here = slice(s, s + w)
        block = factor_rows(jnp.concatenate([a_ref[here, here], eye], axis=1), w)
        both = jnp.concatenate([a_ref[here, :], x_ref[here, :]], axis=1)
        out = jnp.dot(block[:, w:], both, precision=HIGH, preferred_element_type=F32)
        inv_ref[here, :] = out[:, n:]
        if s + w < n:
            change = lax.dot_general(
                out[:, s + w : n], out, FIRST_WITH_FIRST, precision=HIGH, preferred_element_type=F32
            )
            a_ref[s + w :, :] = a_ref[s + w :, :] - change[:, :n]
            x_ref[s + w :, :] = x_ref[s + w :, :] - change[:, n:]


def finish_kernel(col_ref, sums_ref, all_ref, basis_ref, reduced_ref, a_ref, q_ref, x_ref, inv_ref):
    tiles, cols, eight, lanes = sums_ref.shape
    local = basis_ref.shape[0]
    per_matrix = tiles // 2
    halves = a_ref.shape[1] // lanes
    for t in range(tiles):
        target = a_ref if t < per_matrix else q_ref
        block, half = divmod(t % per_matrix, halves)
        for z in range(cols):
            top = z * local + block * eight
            target[top : top + eight, half * lanes : (half + 1) * lanes] = sums_ref[t, z]
    cholesky_inverse(a_ref, x_ref, inv_ref)
    proj = q_ref[...]
    proj = 0.5 * (proj + proj.T)
    inverse = inv_ref[...]
    left = jnp.dot(inverse, proj, precision=HIGH, preferred_element_type=F32)
    reduced_ref[...] = lax.dot_general(
        left, inverse, TRANSPOSED, precision=HIGH, preferred_element_type=F32
    )
    scale = math.sqrt(ALONG_X * ALONG_Y * CORES * basis_ref.shape[1])
    mine = scale * inv_ref[pl.ds(pl.multiple_of(col_ref[0] * local, local), local), :]
    high = mine.astype(BF16)
    low = (mine - high.astype(F32)).astype(BF16)
    states = all_ref[...]
    basis_ref[...] = jnp.dot(high, states, preferred_element_type=F32) + jnp.dot(
        low, states, preferred_element_type=F32
    )


def finish(col, sums, all_states, local):
    total, rows = all_states.shape
    vmem = pl.BlockSpec(memory_space=pltpu.VMEM)
    square = pltpu.VMEM((total, total), F32)
    return pl.pallas_call(
        finish_kernel,
        out_shape=(
            jax.ShapeDtypeStruct((local, rows), F32),
            jax.ShapeDtypeStruct((total, total), F32),
        ),
        in_specs=[pl.BlockSpec(memory_space=pltpu.SMEM), vmem, vmem],
        out_specs=(vmem, vmem),
        scratch_shapes=[square] * 4,
        compiler_params=pltpu.CompilerParams(vmem_limit_bytes=32 * 2**20),
        cost_estimate=pl.CostEstimate(flops=2 * 10**8, bytes_accessed=2**21, transcendentals=0),
    )(col, sums, all_states)


def across_pairs(count):
    pairs = [(i, i + 1 if i % 2 else i - 1) for i in range(count)]
    return [(i, j) for i, j in pairs if 0 <= j < count]


def body(states, diag_blocks, coupling, counts):
    rows = diag_blocks.shape[1]
    local = states.shape[0]
    domains = lax.axis_size(DOM)
    live = (lax.iota(jnp.int32, rows) < counts[0]).astype(F32)[None, :]
    even = lax.axis_index("core") == 0

    def trade(block, onward):
        over = lax.ppermute(jnp.where(even, block, onward), DOM, across_pairs(domains))
        both = lax.all_gather(jnp.where(even, onward, block), "core")
        return over, both

    def apply_op(block):
        low = block.astype(BF16)
        onward = jnp.dot(low, coupling, preferred_element_type=F32)
        over, both = trade(block, onward)
        low, both = lax.optimization_barrier((low, both))
        beside = jnp.where(even, both[1], both[0])
        from_prev, next_block = jnp.where(even, over, beside), jnp.where(even, beside, over)
        own = jnp.dot(low, diag_blocks, preferred_element_type=F32)
        own_t = lax.dot_general(low, diag_blocks, TRANSPOSED, preferred_element_type=F32)
        from_next = lax.dot_general(
            next_block.astype(BF16), coupling, TRANSPOSED, preferred_element_type=F32
        )
        return live * (0.5 * (own + own_t) + from_prev + from_next)

    first = live * states.astype(F32)
    prev = first
    cur = (apply_op(first) - CENTER * first) / HALF
    for step in range(DEGREE - 1):
        prev, cur = cur, 2.0 * (apply_op(cur) - CENTER * cur) / HALF - prev
    filtered = cur.astype(BF16)

    onward = jnp.dot(filtered, coupling, preferred_element_type=F32).astype(BF16)
    arrived = lax.ppermute(onward, DOM, [(i, i + 1) for i in range(domains - 1)])
    cols = lax.axis_size("col")
    all_states = lax.all_to_all(
        jnp.broadcast_to(filtered[None], (cols, local, rows)), "col", 0, 0
    ).reshape(cols * local, rows)
    half_image = jnp.dot(filtered, diag_blocks, preferred_element_type=F32)
    half_image = (half_image + 2.0 * arrived.astype(F32)).astype(BF16)

    total = cols * local
    pair = jnp.concatenate([filtered, half_image], axis=0)
    terms = lax.dot_general(pair, all_states, TRANSPOSED, preferred_element_type=F32)
    tiles = terms.reshape(2 * local // 8, 8, total // 128, 128).transpose(0, 2, 1, 3)
    tiles = tiles.reshape(CORES, ALONG_Y, 8, 128)
    pairs = lax.all_gather(tiles, "core")
    half = lax.dynamic_index_in_dim(pairs, lax.axis_index("core"), 1, keepdims=False).sum(0)
    share = lax.all_to_all(half, "y", 0, 0).sum(0)
    share = lax.all_to_all(jnp.broadcast_to(share, (ALONG_X, 8, 128)), "x", 0, 0).sum(0)
    shares = jnp.broadcast_to(share, (ALONG_Y * cols, 8, 128))
    shares = lax.all_to_all(shares, ("y", "col"), 0, 0)
    sums = lax.all_gather(shares, "core").reshape(CORES * ALONG_Y, cols, 8, 128)
    col = lax.axis_index("col").astype(jnp.int32).reshape(1)
    return finish(col, sums, all_states, local)


def solution(mesh):
    shape = (ALONG_X, ALONG_Y, CORES, mesh.shape["col"])
    fine = Mesh(mesh.devices.reshape(shape), DOM + ("col",))
    placed = (P("col", DOM), P(DOM, None), P(DOM, None), P(DOM))
    return jax.shard_map(
        body, mesh=fine, in_specs=placed, out_specs=(P("col", DOM), P()), check_vma=False
    )
```

```python
import math

import jax
import jax.numpy as jnp
from jax import lax
from jax.experimental import pallas as pl
from jax.experimental.pallas import tpu as pltpu
from jax.sharding import Mesh
from jax.sharding import PartitionSpec as P

DEGREE = 3
HIGH = lax.Precision.HIGHEST
CENTER = 0.5
HALF = 2.0
TRANSPOSED = (((1,), (1,)), ((), ()))
FIRST_WITH_FIRST = (((0,), (0,)), ((), ()))
ALONG_X, ALONG_Y, CORES = 8, 8, 2
DOM = ("x", "y", "core")
WIDE = 64
F32 = jnp.float32
BF16 = jnp.bfloat16


def factor_rows(block, wide):
    done = []
    rest = block
    for start in range(0, wide, 8):
        cols = [
            jnp.broadcast_to(rest[:, start + q : start + q + 1], rest.shape) for q in range(8)
        ]
        rows = [rest[q : q + 1, :] for q in range(8)]
        scaled = []
        for p in range(8):
            pivot = cols[p][p : p + 1, :]
            inv = 1.0 / pivot
            scaled.append(rows[p] * inv)
            for q in range(p + 1, 8):
                link = cols[p][q : q + 1, :]
                rows[q] = rows[q] - link * scaled[p]
                cols[q] = cols[q] - cols[p] * (link * inv)
            done.append(rows[p] * lax.rsqrt(pivot))
        if start + 8 < wide:
            change = cols[0][8:, :] * scaled[0]
            for p in range(1, 8):
                change = change + cols[p][8:, :] * scaled[p]
            rest = rest[8:, :] - change
    return jnp.concatenate(done, axis=0)


def cholesky_inverse(a_ref, x_ref, inv_ref):
    n, w = a_ref.shape[0], WIDE
    i = lax.broadcasted_iota(jnp.int32, (n, n), 0)
    j = lax.broadcasted_iota(jnp.int32, (n, n), 1)
    x_ref[...] = (i == j).astype(F32)
    eye = x_ref[:w, :w]
    for s in range(0, n, w):
        here = slice(s, s + w)
        block = factor_rows(jnp.concatenate([a_ref[here, here], eye], axis=1), w)
        both = jnp.concatenate([a_ref[here, :], x_ref[here, :]], axis=1)
        out = jnp.dot(block[:, w:], both, precision=HIGH, preferred_element_type=F32)
        inv_ref[here, :] = out[:, n:]
        if s + w < n:
            change = lax.dot_general(
                out[:, s + w : n], out, FIRST_WITH_FIRST, precision=HIGH, preferred_element_type=F32
            )
            a_ref[s + w :, :] = a_ref[s + w :, :] - change[:, :n]
            x_ref[s + w :, :] = x_ref[s + w :, :] - change[:, n:]


def finish_kernel(col_ref, sums_ref, all_ref, basis_ref, reduced_ref, a_ref, q_ref, x_ref, inv_ref):
    cores, along, cols, eight, lanes = sums_ref.shape
    local = basis_ref.shape[0]
    tiles = cores * along
    per_matrix = tiles // 2
    halves = a_ref.shape[1] // lanes
    for t in range(tiles):
        target = a_ref if t < per_matrix else q_ref
        block, half = divmod(t % per_matrix, halves)
        for z in range(cols):
            top = z * local + block * eight
            target[top : top + eight, half * lanes : (half + 1) * lanes] = sums_ref[t % cores, t // cores, z]
    cholesky_inverse(a_ref, x_ref, inv_ref)
    proj = q_ref[...]
    proj = 0.5 * (proj + proj.T)
    inverse = inv_ref[...]
    left = jnp.dot(inverse, proj, precision=HIGH, preferred_element_type=F32)
    reduced_ref[...] = lax.dot_general(
        left, inverse, TRANSPOSED, precision=HIGH, preferred_element_type=F32
    )
    scale = math.sqrt(ALONG_X * ALONG_Y * CORES * basis_ref.shape[1])
    mine = scale * inv_ref[pl.ds(pl.multiple_of(col_ref[0] * local, local), local), :]
    high = mine.astype(BF16)
    low = (mine - high.astype(F32)).astype(BF16)
    states = all_ref[...]
    basis_ref[...] = jnp.dot(high, states, preferred_element_type=F32) + jnp.dot(
        low, states, preferred_element_type=F32
    )


def finish(col, sums, all_states, local):
    total, rows = all_states.shape
    vmem = pl.BlockSpec(memory_space=pltpu.VMEM)
    square = pltpu.VMEM((total, total), F32)
    return pl.pallas_call(
        finish_kernel,
        out_shape=(
            jax.ShapeDtypeStruct((local, rows), F32),
            jax.ShapeDtypeStruct((total, total), F32),
        ),
        in_specs=[pl.BlockSpec(memory_space=pltpu.SMEM), vmem, vmem],
        out_specs=(vmem, vmem),
        scratch_shapes=[square] * 4,
        compiler_params=pltpu.CompilerParams(vmem_limit_bytes=32 * 2**20),
        cost_estimate=pl.CostEstimate(flops=2 * 10**8, bytes_accessed=2**21, transcendentals=0),
    )(col, sums, all_states)


def across_pairs(count):
    pairs = [(i, i + 1 if i % 2 else i - 1) for i in range(count)]
    return [(i, j) for i, j in pairs if 0 <= j < count]


def local_kernel(kernel, outs, *operands, scalars=0):
    vmem = pl.BlockSpec(memory_space=pltpu.VMEM)
    smem = pl.BlockSpec(memory_space=pltpu.SMEM)
    return pl.pallas_call(
        kernel,
        out_shape=tuple(jax.ShapeDtypeStruct(shape, dtype) for shape, dtype in outs),
        in_specs=[smem] * scalars + [vmem] * (len(operands) - scalars),
        out_specs=(vmem,) * len(outs),
        compiler_params=pltpu.CompilerParams(vmem_limit_bytes=12 * 2**20),
        cost_estimate=pl.CostEstimate(flops=2**16, bytes_accessed=2**16, transcendentals=0),
    )(*operands)


def live_row(counts_ref, shape):
    return lax.broadcasted_iota(jnp.int32, (1, shape[1]), 1) < counts_ref[0]


def send_off(even, block, low, coupling_ref, over_ref, on_ref):
    onward = jnp.dot(low, coupling_ref[...], preferred_element_type=F32)
    over_ref[...] = jnp.where(even, block, onward)
    on_ref[...] = jnp.where(even, onward, block)


def first_kernel(counts_ref, core_ref, states_ref, coupling_ref, low_ref, over_ref, on_ref):
    live = live_row(counts_ref, states_ref.shape)
    block = jnp.where(live, states_ref[...].astype(F32), 0.0)
    low = block.astype(BF16)
    low_ref[...] = low
    send_off(core_ref[0] == 0, block, low, coupling_ref, over_ref, on_ref)


def own_kernel(low_ref, diag_ref, own_ref):
    low, diag = low_ref[...], diag_ref[...]
    own = jnp.dot(low, diag, preferred_element_type=F32)
    own_t = lax.dot_general(low, diag, TRANSPOSED, preferred_element_type=F32)
    own_ref[...] = 0.5 * (own + own_t)


def recur(counts_ref, even, over_ref, both_ref, own_ref, cur_ref, prev_ref, coupling_ref):
    over = over_ref[...]
    beside = jnp.where(even, both_ref[1], both_ref[0])
    from_prev = jnp.where(even, over, beside)
    next_block = jnp.where(even, beside, over).astype(BF16)
    from_next = lax.dot_general(
        next_block, coupling_ref[...], TRANSPOSED, preferred_element_type=F32
    )
    live = live_row(counts_ref, over.shape)
    image = jnp.where(live, own_ref[...] + from_prev + from_next, 0.0)
    shifted = (image - CENTER * cur_ref[...].astype(F32)) / HALF
    if prev_ref is None:
        return shifted
    return 2.0 * shifted - prev_ref[...].astype(F32)


def step_kernel(counts_ref, core_ref, over_ref, both_ref, own_ref, coupling_ref, cur_ref, *rest):
    prev_ref = rest[0] if len(rest) == 5 else None
    next_ref, low_ref, over_out, on_out = rest[-4:]
    even = core_ref[0] == 0
    block = recur(counts_ref, even, over_ref, both_ref, own_ref, cur_ref, prev_ref, coupling_ref)
    low = block.astype(BF16)
    next_ref[...] = block
    low_ref[...] = low
    send_off(even, block, low, coupling_ref, over_out, on_out)


def last_kernel(
    counts_ref, core_ref, over_ref, both_ref, own_ref, coupling_ref, cur_ref, prev_ref,
    filtered_ref, copies_ref, onward_ref,
):
    even = core_ref[0] == 0
    block = recur(counts_ref, even, over_ref, both_ref, own_ref, cur_ref, prev_ref, coupling_ref)
    low = block.astype(BF16)
    filtered_ref[...] = low
    for z in range(copies_ref.shape[0]):
        copies_ref[z] = low
    onward_ref[...] = jnp.dot(low, coupling_ref[...], preferred_element_type=F32).astype(BF16)


def diag_kernel(filtered_ref, diag_ref, out_ref):
    out_ref[...] = jnp.dot(filtered_ref[...], diag_ref[...], preferred_element_type=F32)


def terms_kernel(filtered_ref, product_ref, arrived_ref, all_ref, tiles_ref):
    half_image = (product_ref[...] + 2.0 * arrived_ref[...].astype(F32)).astype(BF16)
    pair = jnp.concatenate([filtered_ref[...], half_image], axis=0)
    terms = lax.dot_general(pair, all_ref[...], TRANSPOSED, preferred_element_type=F32)
    across = terms.shape[1] // 128
    for t in range(tiles_ref.shape[0]):
        k, half = divmod(t, across)
        tiles_ref[t] = terms[8 * k : 8 * k + 8, 128 * half : 128 * half + 128]


def sum_kernel(parts_ref, copies_ref):
    total = parts_ref[0]
    for i in range(1, parts_ref.shape[0]):
        total = total + parts_ref[i]
    for i in range(copies_ref.shape[0]):
        copies_ref[i] = total


def body(states, diag_blocks, coupling, counts):
    local, rows = states.shape
    block = (local, rows)
    domains, cols = lax.axis_size(DOM), lax.axis_size("col")
    core = lax.axis_index("core").astype(jnp.int32).reshape(1)
    trade = [(block, F32), (block, F32)]

    low, over, on = local_kernel(
        first_kernel, [(block, BF16)] + trade, counts, core, states, coupling, scalars=2
    )
    history = [low]
    for step in range(DEGREE):
        over = lax.ppermute(over, DOM, across_pairs(domains))
        both = lax.all_gather(on, "core")
        low, both = lax.optimization_barrier((low, both))
        (own,) = local_kernel(own_kernel, [(block, F32)], low, diag_blocks)
        args = (counts, core, over, both, own, coupling, *history[:-3:-1])
        if step < DEGREE - 1:
            cur, low, over, on = local_kernel(
                step_kernel, [(block, F32), (block, BF16)] + trade, *args, scalars=2
            )
            history.append(cur)
    filtered, copies, onward = local_kernel(
        last_kernel,
        [(block, BF16), ((cols,) + block, BF16), (block, BF16)],
        *args,
        scalars=2,
    )

    arrived = lax.ppermute(onward, DOM, [(i, i + 1) for i in range(domains - 1)])
    all_states = lax.all_to_all(copies, "col", 0, 0).reshape(cols * local, rows)
    (product,) = local_kernel(diag_kernel, [(block, F32)], filtered, diag_blocks)
    peers = ALONG_Y * CORES
    (tiles,) = local_kernel(
        terms_kernel, [((peers, 8, 128), F32)], filtered, product, arrived, all_states
    )
    parts = lax.all_to_all(tiles, ("y", "core"), 0, 0)
    (copies,) = local_kernel(sum_kernel, [((ALONG_X, 8, 128), F32)], parts)
    parts = lax.all_to_all(copies, "x", 0, 0)
    (copies,) = local_kernel(sum_kernel, [((ALONG_Y * cols, 8, 128), F32)], parts)
    shares = lax.all_to_all(copies, ("y", "col"), 0, 0)
    sums = lax.all_gather(shares, "core").reshape(CORES, ALONG_Y, cols, 8, 128)
    col = lax.axis_index("col").astype(jnp.int32).reshape(1)
    return finish(col, sums, all_states, local)


def solution(mesh):
    shape = (ALONG_X, ALONG_Y, CORES, mesh.shape["col"])
    fine = Mesh(mesh.devices.reshape(shape), DOM + ("col",))
    placed = (P("col", DOM), P(DOM, None), P(DOM, None), P(DOM))
    return jax.shard_map(
        body, mesh=fine, in_specs=placed, out_specs=(P("col", DOM), P()), check_vma=False
    )
```

```python
import math

import jax
import jax.numpy as jnp
from jax import lax
from jax.experimental import pallas as pl
from jax.experimental.pallas import tpu as pltpu
from jax.sharding import Mesh
from jax.sharding import PartitionSpec as P

DEGREE = 3
HIGH = lax.Precision.HIGHEST
CENTER = 0.5
HALF = 2.0
PLAIN = (((1,), (0,)), ((), ()))
TRANSPOSED = (((1,), (1,)), ((), ()))
FIRST_WITH_FIRST = (((0,), (0,)), ((), ()))
ALONG_X, ALONG_Y, CORES = 8, 8, 2
DOM = ("x", "y", "core")
WIDE = 64
EVALUATIONS = 3
CLOSE = 1.6e-5
CHUNKS = 4
F32 = jnp.float32
BF16 = jnp.bfloat16


def factor_rows(block, wide):
    done = []
    rest = block
    for start in range(0, wide, 8):
        cols = [
            jnp.broadcast_to(rest[:, start + q : start + q + 1], rest.shape) for q in range(8)
        ]
        rows = [rest[q : q + 1, :] for q in range(8)]
        scaled = []
        for p in range(8):
            pivot = cols[p][p : p + 1, :]
            inv = 1.0 / pivot
            scaled.append(rows[p] * inv)
            for q in range(p + 1, 8):
                link = cols[p][q : q + 1, :]
                rows[q] = rows[q] - link * scaled[p]
                cols[q] = cols[q] - cols[p] * (link * inv)
            done.append(rows[p] * lax.rsqrt(pivot))
        if start + 8 < wide:
            change = cols[0][8:, :] * scaled[0]
            for p in range(1, 8):
                change = change + cols[p][8:, :] * scaled[p]
            rest = rest[8:, :] - change
    return jnp.concatenate(done, axis=0)


def cholesky_inverse(a_ref, x_ref, inv_ref):
    n, w = a_ref.shape[0], WIDE
    i = lax.broadcasted_iota(jnp.int32, (n, n), 0)
    j = lax.broadcasted_iota(jnp.int32, (n, n), 1)
    x_ref[...] = (i == j).astype(F32)
    eye = x_ref[:w, :w]
    for s in range(0, n, w):
        here = slice(s, s + w)
        block = factor_rows(jnp.concatenate([a_ref[here, here], eye], axis=1), w)
        both = jnp.concatenate([a_ref[here, :], x_ref[here, :]], axis=1)
        out = jnp.dot(block[:, w:], both, precision=HIGH, preferred_element_type=F32)
        inv_ref[here, :] = out[:, n:]
        if s + w < n:
            change = lax.dot_general(
                out[:, s + w : n], out, FIRST_WITH_FIRST, precision=HIGH, preferred_element_type=F32
            )
            a_ref[s + w :, :] = a_ref[s + w :, :] - change[:, :n]
            x_ref[s + w :, :] = x_ref[s + w :, :] - change[:, n:]


def halves(array):
    high = array.astype(BF16)
    return high, (array - high.astype(F32)).astype(BF16)


def product(left, right, dims):
    return lax.dot_general(left, right, dims, preferred_element_type=F32)


def product_of_halves(left, right, dims):
    small = product(left[0], right[1], dims) + product(left[1], right[0], dims)
    return product(left[0], right[0], dims) + small


def newton_inverse(gram, inv_ref):
    n = gram.shape[0]
    i = lax.broadcasted_iota(jnp.int32, (n, n), 0)
    j = lax.broadcasted_iota(jnp.int32, (n, n), 1)
    diagonal = jnp.where(i == j, gram, 0.0)
    down = lax.rsqrt(jnp.sum(diagonal, axis=1, keepdims=True))
    along = lax.rsqrt(jnp.sum(diagonal, axis=0, keepdims=True))
    ident = jnp.where(i == j, 1.0, 0.0)
    weight = jnp.where(i > j, 1.0, 0.5 * ident)
    scaled = jnp.where(i == j, 1.0, gram * down * along)
    parts = halves(scaled)
    x = jnp.where(i > j, -scaled, ident)
    for step in range(EVALUATIONS):
        xs = halves(x)
        if step == 0:
            moved = product(xs[0], parts[0], PLAIN).astype(BF16)
            error = product(moved, xs[0], TRANSPOSED) - ident
        else:
            moved = halves(product_of_halves(xs, parts, PLAIN))
            error = product_of_halves(moved, xs, TRANSPOSED) - ident
        x = x - product((error * weight).astype(BF16), xs[0], PLAIN)
    inv_ref[...] = x * along
    return jnp.sum(error * error)


def finish_kernel(place_ref, sums_ref, all_ref, basis_ref, reduced_ref, a_ref, q_ref, x_ref, inv_ref):
    cores, along, cols, eight, lanes = sums_ref.shape
    local = basis_ref.shape[0]
    tiles = cores * along
    per_matrix = tiles // 2
    across = a_ref.shape[1] // lanes
    for t in range(tiles):
        target = a_ref if t < per_matrix else q_ref
        block, half = divmod(t % per_matrix, across)
        for z in range(cols):
            top = z * local + block * eight
            target[top : top + eight, half * lanes : (half + 1) * lanes] = sums_ref[t % cores, t // cores, z]
    residual = newton_inverse(a_ref[...], inv_ref)

    @pl.when(jnp.logical_not(residual < CLOSE))
    def _():
        cholesky_inverse(a_ref, x_ref, inv_ref)

    proj = q_ref[...]
    inverse = halves(inv_ref[...])
    left = product_of_halves(inverse, halves(0.5 * (proj + proj.T)), PLAIN)
    reduced_ref[...] = product_of_halves(halves(left), inverse, TRANSPOSED)
    scale = math.sqrt(ALONG_X * ALONG_Y * CORES * basis_ref.shape[1])
    mine = scale * inv_ref[pl.ds(pl.multiple_of(place_ref[1] * local, local), local), :]
    high, low = halves(mine)
    states = all_ref[...]
    basis_ref[...] = jnp.dot(high, states, preferred_element_type=F32) + jnp.dot(
        low, states, preferred_element_type=F32
    )


def finish(place, sums, all_states, local):
    total, rows = all_states.shape
    vmem = pl.BlockSpec(memory_space=pltpu.VMEM)
    square = pltpu.VMEM((total, total), F32)
    return pl.pallas_call(
        finish_kernel,
        out_shape=(
            jax.ShapeDtypeStruct((local, rows), F32),
            jax.ShapeDtypeStruct((total, total), F32),
        ),
        in_specs=[pl.BlockSpec(memory_space=pltpu.SMEM), vmem, vmem],
        out_specs=(vmem, vmem),
        scratch_shapes=[square] * 4,
        compiler_params=pltpu.CompilerParams(vmem_limit_bytes=32 * 2**20),
        cost_estimate=pl.CostEstimate(flops=2 * 10**8, bytes_accessed=2**21, transcendentals=0),
    )(place, sums, all_states)


def across_pairs(count):
    pairs = [(i, i + 1 if i % 2 else i - 1) for i in range(count)]
    return [(i, j) for i, j in pairs if 0 <= j < count]


def local_kernel(kernel, outs, *operands, scalars=0):
    vmem = pl.BlockSpec(memory_space=pltpu.VMEM)
    smem = pl.BlockSpec(memory_space=pltpu.SMEM)
    return pl.pallas_call(
        kernel,
        out_shape=tuple(jax.ShapeDtypeStruct(shape, dtype) for shape, dtype in outs),
        in_specs=[smem] * scalars + [vmem] * (len(operands) - scalars),
        out_specs=(vmem,) * len(outs),
        compiler_params=pltpu.CompilerParams(vmem_limit_bytes=12 * 2**20),
        cost_estimate=pl.CostEstimate(flops=2**16, bytes_accessed=2**16, transcendentals=0),
    )(*operands)


def live_row(counts_ref, shape):
    return lax.broadcasted_iota(jnp.int32, (1, shape[1]), 1) < counts_ref[0]


def send_off(even, block, onward, over_ref, on_ref):
    over_ref[...] = jnp.where(even, block, onward)
    on_ref[...] = jnp.where(even, onward, block)


def first_kernel(
    counts_ref, place_ref, states_any, coupling_any, low_ref, over_ref, on_ref,
    states_ref, coupling_ref, sems,
):
    depth = coupling_ref.shape[0] // CHUNKS
    chunks = [pl.ds(k * depth, depth) for k in range(CHUNKS)]
    whole = pltpu.make_async_copy(states_any, states_ref, sems.at[CHUNKS])
    whole.start()
    copies = [
        pltpu.make_async_copy(coupling_any.at[rows], coupling_ref.at[rows], sems.at[k])
        for k, rows in enumerate(chunks)
    ]
    for copy in copies:
        copy.start()
    whole.wait()
    live = live_row(counts_ref, states_ref.shape)
    block = jnp.where(live, states_ref[...].astype(F32), 0.0)
    low = block.astype(BF16)
    low_ref[...] = low
    onward = jnp.zeros_like(block)
    for k, copy in enumerate(copies):
        copy.wait()
        onward = onward + jnp.dot(
            low[:, k * depth : (k + 1) * depth],
            coupling_ref[k * depth : (k + 1) * depth, :],
            preferred_element_type=F32,
        )
    send_off(place_ref[0] == 0, block, onward, over_ref, on_ref)


def first(counts, place, states, coupling):
    block = states.shape
    vmem = pl.BlockSpec(memory_space=pltpu.VMEM)
    smem = pl.BlockSpec(memory_space=pltpu.SMEM)
    left = pl.BlockSpec(memory_space=pltpu.HBM)
    return pl.pallas_call(
        first_kernel,
        out_shape=tuple(jax.ShapeDtypeStruct(block, dtype) for dtype in (BF16, F32, F32)),
        in_specs=[smem, smem, left, left],
        out_specs=(vmem,) * 3,
        scratch_shapes=[
            pltpu.VMEM(block, BF16),
            pltpu.VMEM(coupling.shape, BF16),
            pltpu.SemaphoreType.DMA((CHUNKS + 1,)),
        ],
        compiler_params=pltpu.CompilerParams(vmem_limit_bytes=59 * 2**20),
        cost_estimate=pl.CostEstimate(flops=2**16, bytes_accessed=2**16, transcendentals=0),
    )(counts, place, states, coupling)


def own_kernel(low_ref, diag_ref, own_ref):
    low, diag = low_ref[...], diag_ref[...]
    own = jnp.dot(low, diag, preferred_element_type=F32)
    own_t = lax.dot_general(low, diag, TRANSPOSED, preferred_element_type=F32)
    own_ref[...] = 0.5 * (own + own_t)


def recur(counts_ref, even, over_ref, both_ref, own_ref, cur_ref, prev_ref, coupling_ref):
    over = over_ref[...]
    beside = jnp.where(even, both_ref[1], both_ref[0])
    from_prev = jnp.where(even, over, beside)
    next_block = jnp.where(even, beside, over).astype(BF16)
    from_next = lax.dot_general(
        next_block, coupling_ref[...], TRANSPOSED, preferred_element_type=F32
    )
    live = live_row(counts_ref, over.shape)
    image = jnp.where(live, own_ref[...] + from_prev + from_next, 0.0)
    shifted = (image - CENTER * cur_ref[...].astype(F32)) / HALF
    if prev_ref is None:
        return shifted
    return 2.0 * shifted - prev_ref[...].astype(F32)


def step_kernel(counts_ref, place_ref, over_ref, both_ref, own_ref, coupling_ref, cur_ref, *rest):
    prev_ref = rest[0] if len(rest) == 5 else None
    next_ref, low_ref, over_out, on_out = rest[-4:]
    even = place_ref[0] == 0
    block = recur(counts_ref, even, over_ref, both_ref, own_ref, cur_ref, prev_ref, coupling_ref)
    low = block.astype(BF16)
    next_ref[...] = block
    low_ref[...] = low
    onward = jnp.dot(low, coupling_ref[...], preferred_element_type=F32)
    send_off(even, block, onward, over_out, on_out)


def last_kernel(
    counts_ref, place_ref, over_ref, both_ref, own_ref, coupling_ref, cur_ref, prev_ref,
    filtered_ref, copies_ref, onward_ref,
):
    even = place_ref[0] == 0
    block = recur(counts_ref, even, over_ref, both_ref, own_ref, cur_ref, prev_ref, coupling_ref)
    low = block.astype(BF16)
    filtered_ref[...] = low
    for z in range(copies_ref.shape[0]):
        copies_ref[z] = low
    onward_ref[...] = jnp.dot(low, coupling_ref[...], preferred_element_type=F32).astype(BF16)


def diag_kernel(filtered_ref, diag_ref, out_ref):
    out_ref[...] = jnp.dot(filtered_ref[...], diag_ref[...], preferred_element_type=F32)


def terms_kernel(filtered_ref, product_ref, arrived_ref, all_ref, tiles_ref):
    half_image = (product_ref[...] + 2.0 * arrived_ref[...].astype(F32)).astype(BF16)
    pair = jnp.concatenate([filtered_ref[...], half_image], axis=0)
    terms = lax.dot_general(pair, all_ref[...], TRANSPOSED, preferred_element_type=F32)
    across = terms.shape[1] // 128
    for t in range(tiles_ref.shape[0]):
        k, half = divmod(t, across)
        tiles_ref[t] = terms[8 * k : 8 * k + 8, 128 * half : 128 * half + 128]


def sum_kernel(parts_ref, copies_ref):
    total = parts_ref[0]
    for i in range(1, parts_ref.shape[0]):
        total = total + parts_ref[i]
    for i in range(copies_ref.shape[0]):
        copies_ref[i] = total


def body(states, diag_blocks, coupling, counts):
    local, rows = states.shape
    block = (local, rows)
    domains, cols = lax.axis_size(DOM), lax.axis_size("col")
    place = jnp.stack([lax.axis_index("core"), lax.axis_index("col")]).astype(jnp.int32)
    trade = [(block, F32), (block, F32)]

    low, over, on = first(counts, place, states, coupling)
    history = [low]
    for step in range(DEGREE):
        over = lax.ppermute(over, DOM, across_pairs(domains))
        both = lax.all_gather(on, "core")
        low, both = lax.optimization_barrier((low, both))
        (own,) = local_kernel(own_kernel, [(block, F32)], low, diag_blocks)
        args = (counts, place, over, both, own, coupling, *history[:-3:-1])
        if step < DEGREE - 1:
            cur, low, over, on = local_kernel(
                step_kernel, [(block, F32), (block, BF16)] + trade, *args, scalars=2
            )
            history.append(cur)
    filtered, copies, onward = local_kernel(
        last_kernel,
        [(block, BF16), ((cols,) + block, BF16), (block, BF16)],
        *args,
        scalars=2,
    )

    arrived = lax.ppermute(onward, DOM, [(i, i + 1) for i in range(domains - 1)])
    all_states = lax.all_to_all(copies, "col", 0, 0).reshape(cols * local, rows)
    (product,) = local_kernel(diag_kernel, [(block, F32)], filtered, diag_blocks)
    peers = ALONG_Y * CORES
    (tiles,) = local_kernel(
        terms_kernel, [((peers, 8, 128), F32)], filtered, product, arrived, all_states
    )
    parts = lax.all_to_all(tiles, ("y", "core"), 0, 0)
    (copies,) = local_kernel(sum_kernel, [((ALONG_X, 8, 128), F32)], parts)
    parts = lax.all_to_all(copies, "x", 0, 0)
    (copies,) = local_kernel(sum_kernel, [((ALONG_Y * cols, 8, 128), F32)], parts)
    shares = lax.all_to_all(copies, ("y", "col"), 0, 0)
    sums = lax.all_gather(shares, "core").reshape(CORES, ALONG_Y, cols, 8, 128)
    return finish(place, sums, all_states, local)


def solution(mesh):
    shape = (ALONG_X, ALONG_Y, CORES, mesh.shape["col"])
    fine = Mesh(mesh.devices.reshape(shape), DOM + ("col",))
    placed = (P("col", DOM), P(DOM, None), P(DOM, None), P(DOM))
    return jax.shard_map(
        body, mesh=fine, in_specs=placed, out_specs=(P("col", DOM), P()), check_vma=False
    )
```

```python
import math

import jax
import jax.numpy as jnp
from jax import lax
from jax.experimental import pallas as pl
from jax.experimental.pallas import tpu as pltpu
from jax.sharding import Mesh
from jax.sharding import PartitionSpec as P

DEGREE = 3
HIGH = lax.Precision.HIGHEST
CENTER = 0.5
HALF = 2.0
PLAIN = (((1,), (0,)), ((), ()))
TRANSPOSED = (((1,), (1,)), ((), ()))
FIRST_WITH_FIRST = (((0,), (0,)), ((), ()))
ALONG_X, ALONG_Y, CORES = 8, 8, 2
DOM = ("x", "y", "core")
WIDE = 64
EVALUATIONS = 3
CLOSE = 1.6e-5
F32 = jnp.float32
BF16 = jnp.bfloat16


def factor_rows(block, wide):
    done = []
    rest = block
    for start in range(0, wide, 8):
        cols = [
            jnp.broadcast_to(rest[:, start + q : start + q + 1], rest.shape) for q in range(8)
        ]
        rows = [rest[q : q + 1, :] for q in range(8)]
        scaled = []
        for p in range(8):
            pivot = cols[p][p : p + 1, :]
            inv = 1.0 / pivot
            scaled.append(rows[p] * inv)
            for q in range(p + 1, 8):
                link = cols[p][q : q + 1, :]
                rows[q] = rows[q] - link * scaled[p]
                cols[q] = cols[q] - cols[p] * (link * inv)
            done.append(rows[p] * lax.rsqrt(pivot))
        if start + 8 < wide:
            change = cols[0][8:, :] * scaled[0]
            for p in range(1, 8):
                change = change + cols[p][8:, :] * scaled[p]
            rest = rest[8:, :] - change
    return jnp.concatenate(done, axis=0)


def cholesky_inverse(a_ref, x_ref, inv_ref):
    n, w = a_ref.shape[0], WIDE
    i = lax.broadcasted_iota(jnp.int32, (n, n), 0)
    j = lax.broadcasted_iota(jnp.int32, (n, n), 1)
    x_ref[...] = (i == j).astype(F32)
    eye = x_ref[:w, :w]
    for s in range(0, n, w):
        here = slice(s, s + w)
        block = factor_rows(jnp.concatenate([a_ref[here, here], eye], axis=1), w)
        both = jnp.concatenate([a_ref[here, :], x_ref[here, :]], axis=1)
        out = jnp.dot(block[:, w:], both, precision=HIGH, preferred_element_type=F32)
        inv_ref[here, :] = out[:, n:]
        if s + w < n:
            change = lax.dot_general(
                out[:, s + w : n], out, FIRST_WITH_FIRST, precision=HIGH, preferred_element_type=F32
            )
            a_ref[s + w :, :] = a_ref[s + w :, :] - change[:, :n]
            x_ref[s + w :, :] = x_ref[s + w :, :] - change[:, n:]


def halves(array):
    high = array.astype(BF16)
    return high, (array - high.astype(F32)).astype(BF16)


def product(left, right, dims):
    return lax.dot_general(left, right, dims, preferred_element_type=F32)


def product_of_halves(left, right, dims):
    small = product(left[0], right[1], dims) + product(left[1], right[0], dims)
    return product(left[0], right[0], dims) + small


def newton_inverse(gram, inv_ref):
    n = gram.shape[0]
    i = lax.broadcasted_iota(jnp.int32, (n, n), 0)
    j = lax.broadcasted_iota(jnp.int32, (n, n), 1)
    diagonal = jnp.where(i == j, gram, 0.0)
    down = lax.rsqrt(jnp.sum(diagonal, axis=1, keepdims=True))
    along = lax.rsqrt(jnp.sum(diagonal, axis=0, keepdims=True))
    ident = jnp.where(i == j, 1.0, 0.0)
    weight = jnp.where(i > j, 1.0, 0.5 * ident)
    scaled = jnp.where(i == j, 1.0, gram * down * along)
    parts = halves(scaled)
    x = jnp.where(i > j, -scaled, ident)
    for step in range(EVALUATIONS):
        xs = halves(x)
        if step == 0:
            moved = product(xs[0], parts[0], PLAIN).astype(BF16)
            error = product(moved, xs[0], TRANSPOSED) - ident
        else:
            moved = halves(product_of_halves(xs, parts, PLAIN))
            error = product_of_halves(moved, xs, TRANSPOSED) - ident
        x = x - product((error * weight).astype(BF16), xs[0], PLAIN)
    inv_ref[...] = x * along
    return jnp.sum(error * error)


def finish_kernel(col_ref, sums_ref, all_ref, basis_ref, reduced_ref, a_ref, q_ref, x_ref, inv_ref):
    cores, along, cols, eight, lanes = sums_ref.shape
    local = basis_ref.shape[0]
    tiles = cores * along
    per_matrix = tiles // 2
    across = a_ref.shape[1] // lanes
    for t in range(tiles):
        target = a_ref if t < per_matrix else q_ref
        block, half = divmod(t % per_matrix, across)
        for z in range(cols):
            top = z * local + block * eight
            target[top : top + eight, half * lanes : (half + 1) * lanes] = sums_ref[t % cores, t // cores, z]
    residual = newton_inverse(a_ref[...], inv_ref)

    @pl.when(jnp.logical_not(residual < CLOSE))
    def _():
        cholesky_inverse(a_ref, x_ref, inv_ref)

    proj = q_ref[...]
    inverse = halves(inv_ref[...])
    left = product_of_halves(inverse, halves(0.5 * (proj + proj.T)), PLAIN)
    reduced_ref[...] = product_of_halves(halves(left), inverse, TRANSPOSED)
    scale = math.sqrt(ALONG_X * ALONG_Y * CORES * basis_ref.shape[1])
    mine = scale * inv_ref[pl.ds(pl.multiple_of(col_ref[0] * local, local), local), :]
    high, low = halves(mine)
    states = all_ref[...]
    basis_ref[...] = jnp.dot(high, states, preferred_element_type=F32) + jnp.dot(
        low, states, preferred_element_type=F32
    )


def finish(col, sums, all_states, local):
    total, rows = all_states.shape
    vmem = pl.BlockSpec(memory_space=pltpu.VMEM)
    square = pltpu.VMEM((total, total), F32)
    return pl.pallas_call(
        finish_kernel,
        out_shape=(
            jax.ShapeDtypeStruct((local, rows), F32),
            jax.ShapeDtypeStruct((total, total), F32),
        ),
        in_specs=[pl.BlockSpec(memory_space=pltpu.SMEM), vmem, vmem],
        out_specs=(vmem, vmem),
        scratch_shapes=[square] * 4,
        compiler_params=pltpu.CompilerParams(vmem_limit_bytes=32 * 2**20),
        cost_estimate=pl.CostEstimate(flops=2 * 10**8, bytes_accessed=2**21, transcendentals=0),
    )(col, sums, all_states)


def across_pairs(count):
    pairs = [(i, i + 1 if i % 2 else i - 1) for i in range(count)]
    return [(i, j) for i, j in pairs if 0 <= j < count]


def local_kernel(kernel, outs, *operands, scalars=0):
    vmem = pl.BlockSpec(memory_space=pltpu.VMEM)
    smem = pl.BlockSpec(memory_space=pltpu.SMEM)
    return pl.pallas_call(
        kernel,
        out_shape=tuple(jax.ShapeDtypeStruct(shape, dtype) for shape, dtype in outs),
        in_specs=[smem] * scalars + [vmem] * (len(operands) - scalars),
        out_specs=(vmem,) * len(outs),
        compiler_params=pltpu.CompilerParams(vmem_limit_bytes=12 * 2**20),
        cost_estimate=pl.CostEstimate(flops=2**16, bytes_accessed=2**16, transcendentals=0),
    )(*operands)


def live_row(counts_ref, shape):
    return lax.broadcasted_iota(jnp.int32, (1, shape[1]), 1) < counts_ref[0]


def send_off(even, block, onward, over_ref, on_ref):
    over_ref[...] = jnp.where(even, block, onward)
    on_ref[...] = jnp.where(even, onward, block)


def first_kernel(core_ref, low_ref, coupling_ref, over_ref, on_ref):
    low = low_ref[...]
    onward = jnp.dot(low, coupling_ref[...], preferred_element_type=F32)
    send_off(core_ref[0] == 0, low.astype(F32), onward, over_ref, on_ref)


def own_kernel(low_ref, diag_ref, own_ref):
    low, diag = low_ref[...], diag_ref[...]
    own = jnp.dot(low, diag, preferred_element_type=F32)
    own_t = lax.dot_general(low, diag, TRANSPOSED, preferred_element_type=F32)
    own_ref[...] = 0.5 * (own + own_t)


def recur(counts_ref, even, over_ref, both_ref, own_ref, cur_ref, prev_ref, coupling_ref):
    over = over_ref[...]
    beside = jnp.where(even, both_ref[1], both_ref[0])
    from_prev = jnp.where(even, over, beside)
    next_block = jnp.where(even, beside, over).astype(BF16)
    from_next = lax.dot_general(
        next_block, coupling_ref[...], TRANSPOSED, preferred_element_type=F32
    )
    live = live_row(counts_ref, over.shape)
    image = jnp.where(live, own_ref[...] + from_prev + from_next, 0.0)
    shifted = (image - CENTER * cur_ref[...].astype(F32)) / HALF
    if prev_ref is None:
        return shifted
    return 2.0 * shifted - prev_ref[...].astype(F32)


def step_kernel(counts_ref, core_ref, over_ref, both_ref, own_ref, coupling_ref, cur_ref, *rest):
    prev_ref = rest[0] if len(rest) == 5 else None
    next_ref, low_ref, over_out, on_out = rest[-4:]
    even = core_ref[0] == 0
    block = recur(counts_ref, even, over_ref, both_ref, own_ref, cur_ref, prev_ref, coupling_ref)
    low = block.astype(BF16)
    next_ref[...] = block
    low_ref[...] = low
    onward = jnp.dot(low, coupling_ref[...], preferred_element_type=F32)
    send_off(even, block, onward, over_out, on_out)


def last_kernel(
    counts_ref, core_ref, over_ref, both_ref, own_ref, coupling_ref, cur_ref, prev_ref,
    filtered_ref, copies_ref, onward_ref,
):
    even = core_ref[0] == 0
    block = recur(counts_ref, even, over_ref, both_ref, own_ref, cur_ref, prev_ref, coupling_ref)
    low = block.astype(BF16)
    filtered_ref[...] = low
    for z in range(copies_ref.shape[0]):
        copies_ref[z] = low
    onward_ref[...] = jnp.dot(low, coupling_ref[...], preferred_element_type=F32).astype(BF16)


def diag_kernel(filtered_ref, diag_ref, out_ref):
    out_ref[...] = jnp.dot(filtered_ref[...], diag_ref[...], preferred_element_type=F32)


def terms_kernel(filtered_ref, product_ref, arrived_ref, all_ref, tiles_ref):
    half_image = (product_ref[...] + 2.0 * arrived_ref[...].astype(F32)).astype(BF16)
    pair = jnp.concatenate([filtered_ref[...], half_image], axis=0)
    terms = lax.dot_general(pair, all_ref[...], TRANSPOSED, preferred_element_type=F32)
    across = terms.shape[1] // 128
    for t in range(tiles_ref.shape[0]):
        k, half = divmod(t, across)
        tiles_ref[t] = terms[8 * k : 8 * k + 8, 128 * half : 128 * half + 128]


def sum_kernel(parts_ref, copies_ref):
    total = parts_ref[0]
    for i in range(1, parts_ref.shape[0]):
        total = total + parts_ref[i]
    for i in range(copies_ref.shape[0]):
        copies_ref[i] = total


def body(states, diag_blocks, coupling, counts):
    local, rows = states.shape
    block = (local, rows)
    domains, cols = lax.axis_size(DOM), lax.axis_size("col")
    core = lax.axis_index("core").astype(jnp.int32).reshape(1)
    col = lax.axis_index("col").astype(jnp.int32).reshape(1)
    trade = [(block, F32), (block, F32)]

    live = lax.iota(jnp.int32, rows) < counts[0]
    low = jnp.where(live[None, :], states, jnp.zeros_like(states))
    over, on = local_kernel(first_kernel, trade, core, low, coupling, scalars=1)
    history = [low]
    for step in range(DEGREE):
        over = lax.ppermute(over, DOM, across_pairs(domains))
        both = lax.all_gather(on, "core")
        low, both, col = lax.optimization_barrier((low, both, col))
        (own,) = local_kernel(own_kernel, [(block, F32)], low, diag_blocks)
        args = (counts, core, over, both, own, coupling, *history[:-3:-1])
        if step < DEGREE - 1:
            cur, low, over, on = local_kernel(
                step_kernel, [(block, F32), (block, BF16)] + trade, *args, scalars=2
            )
            history.append(cur)
    filtered, copies, onward = local_kernel(
        last_kernel,
        [(block, BF16), ((cols,) + block, BF16), (block, BF16)],
        *args,
        scalars=2,
    )

    arrived = lax.ppermute(onward, DOM, [(i, i + 1) for i in range(domains - 1)])
    all_states = lax.all_to_all(copies, "col", 0, 0).reshape(cols * local, rows)
    (product,) = local_kernel(diag_kernel, [(block, F32)], filtered, diag_blocks)
    peers = ALONG_Y * CORES
    (tiles,) = local_kernel(
        terms_kernel, [((peers, 8, 128), F32)], filtered, product, arrived, all_states
    )
    parts = lax.all_to_all(tiles, ("y", "core"), 0, 0)
    (copies,) = local_kernel(sum_kernel, [((ALONG_X, 8, 128), F32)], parts)
    parts = lax.all_to_all(copies, "x", 0, 0)
    (copies,) = local_kernel(sum_kernel, [((ALONG_Y * cols, 8, 128), F32)], parts)
    shares = lax.all_to_all(copies, ("y", "col"), 0, 0)
    sums = lax.all_gather(shares, "core").reshape(CORES, ALONG_Y, cols, 8, 128)
    return finish(col, sums, all_states, local)


def solution(mesh):
    shape = (ALONG_X, ALONG_Y, CORES, mesh.shape["col"])
    fine = Mesh(mesh.devices.reshape(shape), DOM + ("col",))
    placed = (P("col", DOM), P(DOM, None), P(DOM, None), P(DOM))
    return jax.shard_map(
        body, mesh=fine, in_specs=placed, out_specs=(P("col", DOM), P()), check_vma=False
    )
```

```python
import math

import jax
import jax.numpy as jnp
from jax import lax
from jax.experimental import pallas as pl
from jax.experimental.pallas import tpu as pltpu
from jax.sharding import Mesh
from jax.sharding import PartitionSpec as P

DEGREE = 3
HIGH = lax.Precision.HIGHEST
CENTER = 0.5
HALF = 2.0
PLAIN = (((1,), (0,)), ((), ()))
TRANSPOSED = (((1,), (1,)), ((), ()))
FIRST_WITH_FIRST = (((0,), (0,)), ((), ()))
ALONG_X, ALONG_Y, CORES = 8, 8, 2
DOM = ("x", "y", "core")
WIDE = 64
EVALUATIONS = 3
CLOSE = 1.6e-5
CHUNKS = 4
F32 = jnp.float32
BF16 = jnp.bfloat16


def factor_rows(block, wide):
    done = []
    rest = block
    for start in range(0, wide, 8):
        cols = [
            jnp.broadcast_to(rest[:, start + q : start + q + 1], rest.shape) for q in range(8)
        ]
        rows = [rest[q : q + 1, :] for q in range(8)]
        scaled = []
        for p in range(8):
            pivot = cols[p][p : p + 1, :]
            inv = 1.0 / pivot
            scaled.append(rows[p] * inv)
            for q in range(p + 1, 8):
                link = cols[p][q : q + 1, :]
                rows[q] = rows[q] - link * scaled[p]
                cols[q] = cols[q] - cols[p] * (link * inv)
            done.append(rows[p] * lax.rsqrt(pivot))
        if start + 8 < wide:
            change = cols[0][8:, :] * scaled[0]
            for p in range(1, 8):
                change = change + cols[p][8:, :] * scaled[p]
            rest = rest[8:, :] - change
    return jnp.concatenate(done, axis=0)


def cholesky_inverse(a_ref, x_ref, inv_ref):
    n, w = a_ref.shape[0], WIDE
    i = lax.broadcasted_iota(jnp.int32, (n, n), 0)
    j = lax.broadcasted_iota(jnp.int32, (n, n), 1)
    x_ref[...] = (i == j).astype(F32)
    eye = x_ref[:w, :w]
    for s in range(0, n, w):
        here = slice(s, s + w)
        block = factor_rows(jnp.concatenate([a_ref[here, here], eye], axis=1), w)
        both = jnp.concatenate([a_ref[here, :], x_ref[here, :]], axis=1)
        out = jnp.dot(block[:, w:], both, precision=HIGH, preferred_element_type=F32)
        inv_ref[here, :] = out[:, n:]
        if s + w < n:
            change = lax.dot_general(
                out[:, s + w : n], out, FIRST_WITH_FIRST, precision=HIGH, preferred_element_type=F32
            )
            a_ref[s + w :, :] = a_ref[s + w :, :] - change[:, :n]
            x_ref[s + w :, :] = x_ref[s + w :, :] - change[:, n:]


def halves(array):
    high = array.astype(BF16)
    return high, (array - high.astype(F32)).astype(BF16)


def product(left, right, dims):
    return lax.dot_general(left, right, dims, preferred_element_type=F32)


def product_of_halves(left, right, dims):
    small = product(left[0], right[1], dims) + product(left[1], right[0], dims)
    return product(left[0], right[0], dims) + small


def newton_inverse(gram, inv_ref):
    n = gram.shape[0]
    i = lax.broadcasted_iota(jnp.int32, (n, n), 0)
    j = lax.broadcasted_iota(jnp.int32, (n, n), 1)
    diagonal = jnp.where(i == j, gram, 0.0)
    down = lax.rsqrt(jnp.sum(diagonal, axis=1, keepdims=True))
    along = lax.rsqrt(jnp.sum(diagonal, axis=0, keepdims=True))
    ident = jnp.where(i == j, 1.0, 0.0)
    weight = jnp.where(i > j, 1.0, 0.5 * ident)
    scaled = jnp.where(i == j, 1.0, gram * down * along)
    parts = halves(scaled)
    x = jnp.where(i > j, -scaled, ident)
    for step in range(EVALUATIONS):
        xs = halves(x)
        if step == 0:
            moved = product(xs[0], parts[0], PLAIN).astype(BF16)
            error = product(moved, xs[0], TRANSPOSED) - ident
        else:
            moved = halves(product_of_halves(xs, parts, PLAIN))
            error = product_of_halves(moved, xs, TRANSPOSED) - ident
        x = x - product((error * weight).astype(BF16), xs[0], PLAIN)
    inv_ref[...] = x * along
    return jnp.sum(error * error)


def finish_kernel(col_ref, sums_ref, all_ref, basis_ref, reduced_ref, a_ref, q_ref, x_ref, inv_ref):
    cores, along, cols, eight, lanes = sums_ref.shape
    local = basis_ref.shape[0]
    tiles = cores * along
    per_matrix = tiles // 2
    across = a_ref.shape[1] // lanes
    for t in range(tiles):
        target = a_ref if t < per_matrix else q_ref
        block, half = divmod(t % per_matrix, across)
        for z in range(cols):
            top = z * local + block * eight
            target[top : top + eight, half * lanes : (half + 1) * lanes] = sums_ref[t % cores, t // cores, z]
    residual = newton_inverse(a_ref[...], inv_ref)

    @pl.when(jnp.logical_not(residual < CLOSE))
    def _():
        cholesky_inverse(a_ref, x_ref, inv_ref)

    proj = q_ref[...]
    inverse = halves(inv_ref[...])
    left = product_of_halves(inverse, halves(0.5 * (proj + proj.T)), PLAIN)
    reduced_ref[...] = product_of_halves(halves(left), inverse, TRANSPOSED)
    scale = math.sqrt(ALONG_X * ALONG_Y * CORES * basis_ref.shape[1])
    mine = scale * inv_ref[pl.ds(pl.multiple_of(col_ref[0] * local, local), local), :]
    high, low = halves(mine)
    states = all_ref[...]
    basis_ref[...] = jnp.dot(high, states, preferred_element_type=F32) + jnp.dot(
        low, states, preferred_element_type=F32
    )


def finish(col, sums, all_states, local):
    total, rows = all_states.shape
    vmem = pl.BlockSpec(memory_space=pltpu.VMEM)
    square = pltpu.VMEM((total, total), F32)
    return pl.pallas_call(
        finish_kernel,
        out_shape=(
            jax.ShapeDtypeStruct((local, rows), F32),
            jax.ShapeDtypeStruct((total, total), F32),
        ),
        in_specs=[pl.BlockSpec(memory_space=pltpu.SMEM), vmem, vmem],
        out_specs=(vmem, vmem),
        scratch_shapes=[square] * 4,
        compiler_params=pltpu.CompilerParams(vmem_limit_bytes=32 * 2**20),
        cost_estimate=pl.CostEstimate(flops=2 * 10**8, bytes_accessed=2**21, transcendentals=0),
    )(col, sums, all_states)


def across_pairs(count):
    pairs = [(i, i + 1 if i % 2 else i - 1) for i in range(count)]
    return [(i, j) for i, j in pairs if 0 <= j < count]


def local_kernel(kernel, outs, *operands, scalars=0):
    vmem = pl.BlockSpec(memory_space=pltpu.VMEM)
    smem = pl.BlockSpec(memory_space=pltpu.SMEM)
    return pl.pallas_call(
        kernel,
        out_shape=tuple(jax.ShapeDtypeStruct(shape, dtype) for shape, dtype in outs),
        in_specs=[smem] * scalars + [vmem] * (len(operands) - scalars),
        out_specs=(vmem,) * len(outs),
        compiler_params=pltpu.CompilerParams(vmem_limit_bytes=12 * 2**20),
        cost_estimate=pl.CostEstimate(flops=2**16, bytes_accessed=2**16, transcendentals=0),
    )(*operands)


def live_row(counts_ref, shape):
    return lax.broadcasted_iota(jnp.int32, (1, shape[1]), 1) < counts_ref[0]


def send_off(even, block, onward, over_ref, on_ref):
    over_ref[...] = jnp.where(even, block, onward)
    on_ref[...] = jnp.where(even, onward, block)


def chunked(whole_hbm, whole_ref, array_hbm, array_ref, sems):
    depth = array_ref.shape[0] // CHUNKS
    chunks = [pl.ds(k * depth, depth) for k in range(CHUNKS)]
    whole = pltpu.make_async_copy(whole_hbm, whole_ref, sems.at[CHUNKS])
    whole.start()
    copies = [
        pltpu.make_async_copy(array_hbm.at[rows], array_ref.at[rows], sems.at[k])
        for k, rows in enumerate(chunks)
    ]
    for copy in copies:
        copy.start()
    whole.wait()
    return [(copy, slice(k * depth, (k + 1) * depth)) for k, copy in enumerate(copies)]


def first_kernel(
    counts_ref, core_ref, states_hbm, coupling_hbm, low_ref, over_ref, on_ref,
    states_ref, coupling_ref, sems,
):
    copies = chunked(states_hbm, states_ref, coupling_hbm, coupling_ref, sems)
    live = live_row(counts_ref, states_ref.shape)
    block = jnp.where(live, states_ref[...].astype(F32), 0.0)
    low = block.astype(BF16)
    low_ref[...] = low
    onward = jnp.zeros_like(block)
    for copy, rows in copies:
        copy.wait()
        onward = onward + jnp.dot(
            low[:, rows], coupling_ref[rows, :], preferred_element_type=F32
        )
    send_off(core_ref[0] == 0, block, onward, over_ref, on_ref)


def first_own_kernel(low_any, diag_ref, own_ref, low_ref, sem):
    copy = pltpu.make_async_copy(low_any, low_ref, sem)
    copy.start()
    copy.wait()
    own_kernel(low_ref, diag_ref, own_ref)


def first_step(counts, core, states, coupling):
    block = states.shape
    vmem = pl.BlockSpec(memory_space=pltpu.VMEM)
    smem = pl.BlockSpec(memory_space=pltpu.SMEM)
    left = pl.BlockSpec(memory_space=pltpu.HBM)
    return pl.pallas_call(
        first_kernel,
        out_shape=tuple(jax.ShapeDtypeStruct(block, dtype) for dtype in (BF16, F32, F32)),
        in_specs=[smem, smem, left, left],
        out_specs=(vmem,) * 3,
        scratch_shapes=[
            pltpu.VMEM(block, BF16),
            pltpu.VMEM(coupling.shape, BF16),
            pltpu.SemaphoreType.DMA((CHUNKS + 1,)),
        ],
        compiler_params=pltpu.CompilerParams(vmem_limit_bytes=62 * 2**20),
        cost_estimate=pl.CostEstimate(flops=2**16, bytes_accessed=2**16, transcendentals=0),
    )(counts, core, states, coupling)


def first_own(low, diag_blocks):
    return pl.pallas_call(
        first_own_kernel,
        out_shape=jax.ShapeDtypeStruct(low.shape, F32),
        in_specs=[
            pl.BlockSpec(memory_space=pl.ANY),
            pl.BlockSpec(memory_space=pltpu.VMEM),
        ],
        out_specs=pl.BlockSpec(memory_space=pltpu.VMEM),
        scratch_shapes=[pltpu.VMEM(low.shape, BF16), pltpu.SemaphoreType.DMA],
        compiler_params=pltpu.CompilerParams(vmem_limit_bytes=12 * 2**20),
        cost_estimate=pl.CostEstimate(flops=2**16, bytes_accessed=2**16, transcendentals=0),
    )(low, diag_blocks)


def own_kernel(low_ref, diag_ref, own_ref):
    low, diag = low_ref[...], diag_ref[...]
    own = jnp.dot(low, diag, preferred_element_type=F32)
    own_t = lax.dot_general(low, diag, TRANSPOSED, preferred_element_type=F32)
    own_ref[...] = 0.5 * (own + own_t)


def recur(counts_ref, even, over_ref, both_ref, own_ref, cur_ref, prev_ref, coupling_ref):
    over = over_ref[...]
    beside = jnp.where(even, both_ref[1], both_ref[0])
    from_prev = jnp.where(even, over, beside)
    next_block = jnp.where(even, beside, over).astype(BF16)
    from_next = lax.dot_general(
        next_block, coupling_ref[...], TRANSPOSED, preferred_element_type=F32
    )
    live = live_row(counts_ref, over.shape)
    image = jnp.where(live, own_ref[...] + from_prev + from_next, 0.0)
    shifted = (image - CENTER * cur_ref[...].astype(F32)) / HALF
    if prev_ref is None:
        return shifted
    return 2.0 * shifted - prev_ref[...].astype(F32)


def step_kernel(counts_ref, core_ref, over_ref, both_ref, own_ref, coupling_ref, cur_ref, *rest):
    prev_ref = rest[0] if len(rest) == 5 else None
    next_ref, low_ref, over_out, on_out = rest[-4:]
    even = core_ref[0] == 0
    block = recur(counts_ref, even, over_ref, both_ref, own_ref, cur_ref, prev_ref, coupling_ref)
    low = block.astype(BF16)
    next_ref[...] = block
    low_ref[...] = low
    onward = jnp.dot(low, coupling_ref[...], preferred_element_type=F32)
    send_off(even, block, onward, over_out, on_out)


def last_kernel(
    counts_ref, core_ref, over_ref, both_ref, own_ref, coupling_ref, cur_ref, prev_ref,
    filtered_ref, copies_ref,
):
    even = core_ref[0] == 0
    block = recur(counts_ref, even, over_ref, both_ref, own_ref, cur_ref, prev_ref, coupling_ref)
    low = block.astype(BF16)
    filtered_ref[...] = low
    for z in range(copies_ref.shape[0]):
        copies_ref[z] = low


def product_kernel(left_ref, right_ref, out_ref):
    out = jnp.dot(left_ref[...], right_ref[...], preferred_element_type=F32)
    out_ref[...] = out.astype(out_ref.dtype)


def terms_kernel(filtered_ref, product_ref, arrived_ref, all_ref, tiles_ref):
    half_image = (product_ref[...] + 2.0 * arrived_ref[...].astype(F32)).astype(BF16)
    pair = jnp.concatenate([filtered_ref[...], half_image], axis=0)
    terms = lax.dot_general(pair, all_ref[...], TRANSPOSED, preferred_element_type=F32)
    across = terms.shape[1] // 128
    for t in range(tiles_ref.shape[0]):
        k, half = divmod(t, across)
        tiles_ref[t] = terms[8 * k : 8 * k + 8, 128 * half : 128 * half + 128]


def sum_kernel(parts_ref, copies_ref):
    total = parts_ref[0]
    for i in range(1, parts_ref.shape[0]):
        total = total + parts_ref[i]
    for i in range(copies_ref.shape[0]):
        copies_ref[i] = total


def body(states, diag_blocks, coupling, counts):
    local, rows = states.shape
    block = (local, rows)
    domains, cols = lax.axis_size(DOM), lax.axis_size("col")
    core = lax.axis_index("core").astype(jnp.int32).reshape(1)
    col = lax.axis_index("col").astype(jnp.int32).reshape(1)
    trade = [(block, F32), (block, F32)]

    low, over, on = first_step(counts, core, states, coupling)
    history = [low]
    for step in range(DEGREE):
        over = lax.ppermute(over, DOM, across_pairs(domains))
        both = lax.all_gather(on, "core")
        low, both, col = lax.optimization_barrier((low, both, col))
        if step == 0:
            own = first_own(low, diag_blocks)
        else:
            (own,) = local_kernel(own_kernel, [(block, F32)], low, diag_blocks)
        args = (counts, core, over, both, own, coupling, *history[:-3:-1])
        if step < DEGREE - 1:
            cur, low, over, on = local_kernel(
                step_kernel, [(block, F32), (block, BF16)] + trade, *args, scalars=2
            )
            history.append(cur)
    filtered, copies = local_kernel(
        last_kernel, [(block, BF16), ((cols,) + block, BF16)], *args, scalars=2
    )

    (onward,) = local_kernel(product_kernel, [(block, BF16)], filtered, coupling)
    arrived = lax.ppermute(onward, DOM, [(i, i + 1) for i in range(domains - 1)])
    all_states = lax.all_to_all(copies, "col", 0, 0).reshape(cols * local, rows)
    (product,) = local_kernel(product_kernel, [(block, F32)], filtered, diag_blocks)
    peers = ALONG_Y * CORES
    (tiles,) = local_kernel(
        terms_kernel, [((peers, 8, 128), F32)], filtered, product, arrived, all_states
    )
    parts = lax.all_to_all(tiles, ("y", "core"), 0, 0)
    (copies,) = local_kernel(sum_kernel, [((ALONG_X, 8, 128), F32)], parts)
    parts = lax.all_to_all(copies, "x", 0, 0)
    (copies,) = local_kernel(sum_kernel, [((ALONG_Y * cols, 8, 128), F32)], parts)
    shares = lax.all_to_all(copies, ("y", "col"), 0, 0)
    sums = lax.all_gather(shares, "core").reshape(CORES, ALONG_Y, cols, 8, 128)
    return finish(col, sums, all_states, local)


def solution(mesh):
    shape = (ALONG_X, ALONG_Y, CORES, mesh.shape["col"])
    fine = Mesh(mesh.devices.reshape(shape), DOM + ("col",))
    placed = (P("col", DOM), P(DOM, None), P(DOM, None), P(DOM))
    return jax.shard_map(
        body, mesh=fine, in_specs=placed, out_specs=(P("col", DOM), P()), check_vma=False
    )
```

```python
import math

import jax
import jax.numpy as jnp
from jax import lax
from jax.experimental import pallas as pl
from jax.experimental.pallas import tpu as pltpu
from jax.sharding import Mesh
from jax.sharding import PartitionSpec as P

DEGREE = 3
HIGH = lax.Precision.HIGHEST
CENTER = 0.5
HALF = 2.0
PLAIN = (((1,), (0,)), ((), ()))
TRANSPOSED = (((1,), (1,)), ((), ()))
FIRST_WITH_FIRST = (((0,), (0,)), ((), ()))
ALONG_X, ALONG_Y, CORES = 8, 8, 2
DOM = ("x", "y", "core")
WIDE = 64
EVALUATIONS = 3
CLOSE = 1.6e-5
F32 = jnp.float32
BF16 = jnp.bfloat16


def factor_rows(block, wide):
    done = []
    rest = block
    for start in range(0, wide, 8):
        cols = [
            jnp.broadcast_to(rest[:, start + q : start + q + 1], rest.shape) for q in range(8)
        ]
        rows = [rest[q : q + 1, :] for q in range(8)]
        scaled = []
        for p in range(8):
            pivot = cols[p][p : p + 1, :]
            inv = 1.0 / pivot
            scaled.append(rows[p] * inv)
            for q in range(p + 1, 8):
                link = cols[p][q : q + 1, :]
                rows[q] = rows[q] - link * scaled[p]
                cols[q] = cols[q] - cols[p] * (link * inv)
            done.append(rows[p] * lax.rsqrt(pivot))
        if start + 8 < wide:
            change = cols[0][8:, :] * scaled[0]
            for p in range(1, 8):
                change = change + cols[p][8:, :] * scaled[p]
            rest = rest[8:, :] - change
    return jnp.concatenate(done, axis=0)


def cholesky_inverse(a_ref, x_ref, inv_ref):
    n, w = a_ref.shape[0], WIDE
    i = lax.broadcasted_iota(jnp.int32, (n, n), 0)
    j = lax.broadcasted_iota(jnp.int32, (n, n), 1)
    x_ref[...] = (i == j).astype(F32)
    eye = x_ref[:w, :w]
    for s in range(0, n, w):
        here = slice(s, s + w)
        block = factor_rows(jnp.concatenate([a_ref[here, here], eye], axis=1), w)
        both = jnp.concatenate([a_ref[here, :], x_ref[here, :]], axis=1)
        out = jnp.dot(block[:, w:], both, precision=HIGH, preferred_element_type=F32)
        inv_ref[here, :] = out[:, n:]
        if s + w < n:
            change = lax.dot_general(
                out[:, s + w : n], out, FIRST_WITH_FIRST, precision=HIGH, preferred_element_type=F32
            )
            a_ref[s + w :, :] = a_ref[s + w :, :] - change[:, :n]
            x_ref[s + w :, :] = x_ref[s + w :, :] - change[:, n:]


def halves(array):
    high = array.astype(BF16)
    return high, (array - high.astype(F32)).astype(BF16)


def product(left, right, dims):
    return lax.dot_general(left, right, dims, preferred_element_type=F32)


def product_of_halves(left, right, dims):
    small = product(left[0], right[1], dims) + product(left[1], right[0], dims)
    return product(left[0], right[0], dims) + small


def newton_inverse(gram, inv_ref):
    n = gram.shape[0]
    i = lax.broadcasted_iota(jnp.int32, (n, n), 0)
    j = lax.broadcasted_iota(jnp.int32, (n, n), 1)
    diagonal = jnp.where(i == j, gram, 0.0)
    down = lax.rsqrt(jnp.sum(diagonal, axis=1, keepdims=True))
    along = lax.rsqrt(jnp.sum(diagonal, axis=0, keepdims=True))
    ident = jnp.where(i == j, 1.0, 0.0)
    weight = jnp.where(i > j, 1.0, 0.5 * ident)
    scaled = jnp.where(i == j, 1.0, gram * down * along)
    parts = halves(scaled)
    x = jnp.where(i > j, -scaled, ident)
    for step in range(EVALUATIONS):
        xs = halves(x)
        if step == 0:
            moved = product(xs[0], parts[0], PLAIN).astype(BF16)
            error = product(moved, xs[0], TRANSPOSED) - ident
        else:
            moved = halves(product_of_halves(xs, parts, PLAIN))
            error = product_of_halves(moved, xs, TRANSPOSED) - ident
        x = x - product((error * weight).astype(BF16), xs[0], PLAIN)
    inv_ref[...] = x * along
    return jnp.sum(error * error)


def finish_kernel(col_ref, sums_ref, all_ref, basis_ref, reduced_ref, a_ref, q_ref, x_ref, inv_ref):
    cores, along, cols, eight, lanes = sums_ref.shape
    local = basis_ref.shape[0]
    tiles = cores * along
    per_matrix = tiles // 2
    across = a_ref.shape[1] // lanes
    for t in range(tiles):
        target = a_ref if t < per_matrix else q_ref
        block, half = divmod(t % per_matrix, across)
        for z in range(cols):
            top = z * local + block * eight
            target[top : top + eight, half * lanes : (half + 1) * lanes] = sums_ref[t % cores, t // cores, z]
    residual = newton_inverse(a_ref[...], inv_ref)

    @pl.when(jnp.logical_not(residual < CLOSE))
    def _():
        cholesky_inverse(a_ref, x_ref, inv_ref)

    proj = q_ref[...]
    inverse = halves(inv_ref[...])
    left = product_of_halves(inverse, halves(0.5 * (proj + proj.T)), PLAIN)
    reduced_ref[...] = product_of_halves(halves(left), inverse, TRANSPOSED)
    scale = math.sqrt(ALONG_X * ALONG_Y * CORES * basis_ref.shape[1])
    mine = scale * inv_ref[pl.ds(pl.multiple_of(col_ref[0] * local, local), local), :]
    high, low = halves(mine)
    states = all_ref[...]
    basis_ref[...] = jnp.dot(high, states, preferred_element_type=F32) + jnp.dot(
        low, states, preferred_element_type=F32
    )


def finish(col, sums, all_states, local):
    total, rows = all_states.shape
    vmem = pl.BlockSpec(memory_space=pltpu.VMEM)
    square = pltpu.VMEM((total, total), F32)
    return pl.pallas_call(
        finish_kernel,
        out_shape=(
            jax.ShapeDtypeStruct((local, rows), F32),
            jax.ShapeDtypeStruct((total, total), F32),
        ),
        in_specs=[pl.BlockSpec(memory_space=pltpu.SMEM), vmem, vmem],
        out_specs=(vmem, vmem),
        scratch_shapes=[square] * 4,
        compiler_params=pltpu.CompilerParams(vmem_limit_bytes=32 * 2**20),
        cost_estimate=pl.CostEstimate(flops=2 * 10**8, bytes_accessed=2**21, transcendentals=0),
    )(col, sums, all_states)


def across_pairs(count):
    pairs = [(i, i + 1 if i % 2 else i - 1) for i in range(count)]
    return [(i, j) for i, j in pairs if 0 <= j < count]


def local_kernel(kernel, outs, *operands, scalars=0):
    vmem = pl.BlockSpec(memory_space=pltpu.VMEM)
    smem = pl.BlockSpec(memory_space=pltpu.SMEM)
    return pl.pallas_call(
        kernel,
        out_shape=tuple(jax.ShapeDtypeStruct(shape, dtype) for shape, dtype in outs),
        in_specs=[smem] * scalars + [vmem] * (len(operands) - scalars),
        out_specs=(vmem,) * len(outs),
        compiler_params=pltpu.CompilerParams(vmem_limit_bytes=12 * 2**20),
        cost_estimate=pl.CostEstimate(flops=2**16, bytes_accessed=2**16, transcendentals=0),
    )(*operands)


def own_kernel(low_ref, diag_ref, own_ref):
    low, diag = low_ref[...], diag_ref[...]
    own = jnp.dot(low, diag, preferred_element_type=F32)
    own_t = lax.dot_general(low, diag, TRANSPOSED, preferred_element_type=F32)
    own_ref[...] = 0.5 * (own + own_t)


def copies_kernel(array_ref, copies_hbm, sems):
    copies = [
        pltpu.make_async_copy(array_ref, copies_hbm.at[i], sems.at[i])
        for i in range(copies_hbm.shape[0])
    ]
    for copy in copies:
        copy.start()
    for copy in copies:
        copy.wait()


def copied(array, count):
    return pl.pallas_call(
        copies_kernel,
        out_shape=jax.ShapeDtypeStruct((count,) + array.shape, array.dtype),
        in_specs=[pl.BlockSpec(memory_space=pltpu.VMEM)],
        out_specs=pl.BlockSpec(memory_space=pltpu.HBM),
        scratch_shapes=[pltpu.SemaphoreType.DMA((count,))],
        compiler_params=pltpu.CompilerParams(vmem_limit_bytes=12 * 2**20),
        cost_estimate=pl.CostEstimate(flops=0, bytes_accessed=2**16, transcendentals=0),
    )(array)


def product_kernel(left_ref, right_ref, out_ref):
    out = jnp.dot(left_ref[...], right_ref[...], preferred_element_type=F32)
    out_ref[...] = out.astype(out_ref.dtype)


def terms_kernel(filtered_ref, product_ref, arrived_ref, all_ref, tiles_ref):
    half_image = (product_ref[...] + 2.0 * arrived_ref[...].astype(F32)).astype(BF16)
    pair = jnp.concatenate([filtered_ref[...], half_image], axis=0)
    terms = lax.dot_general(pair, all_ref[...], TRANSPOSED, preferred_element_type=F32)
    across = terms.shape[1] // 128
    for t in range(tiles_ref.shape[0]):
        k, half = divmod(t, across)
        tiles_ref[t] = terms[8 * k : 8 * k + 8, 128 * half : 128 * half + 128]


def sum_kernel(parts_ref, copies_ref):
    total = parts_ref[0]
    for i in range(1, parts_ref.shape[0]):
        total = total + parts_ref[i]
    for i in range(copies_ref.shape[0]):
        copies_ref[i] = total


def body(states, diag_blocks, coupling, counts):
    local, rows = states.shape
    block = (local, rows)
    domains, cols = lax.axis_size(DOM), lax.axis_size("col")
    core = lax.axis_index("core").astype(jnp.int32).reshape(1)
    col = lax.axis_index("col").astype(jnp.int32).reshape(1)

    live = (lax.iota(jnp.int32, rows) < counts[0])[None, :]
    low = lax.optimization_barrier(jnp.where(live, states, jnp.zeros_like(states)))
    even = core[0] == 0
    history = [low.astype(F32)]
    for step in range(DEGREE):
        onward = jnp.dot(low, coupling, preferred_element_type=F32)
        over = jnp.where(even, history[-1], onward)
        on = jnp.where(even, onward, history[-1])
        over = lax.ppermute(over, DOM, across_pairs(domains))
        both = lax.all_gather(on, "core")
        low, both, col = lax.optimization_barrier((low, both, col))
        (own,) = local_kernel(own_kernel, [(block, F32)], low, diag_blocks)
        beside = jnp.where(even, both[1], both[0])
        next_block = jnp.where(even, beside, over).astype(BF16)
        from_next = lax.dot_general(
            next_block, coupling, TRANSPOSED, preferred_element_type=F32
        )
        image = jnp.where(live, own + jnp.where(even, over, beside) + from_next, 0.0)
        cur = (image - CENTER * history[-1]) / HALF
        if step > 0:
            cur = 2.0 * cur - history[-2]
        history.append(cur)
        low = cur.astype(BF16)
    filtered = lax.optimization_barrier(low)
    copies = copied(filtered, cols)

    onward = jnp.dot(filtered, coupling, preferred_element_type=F32).astype(BF16)
    arrived = lax.ppermute(onward, DOM, [(i, i + 1) for i in range(domains - 1)])
    all_states = lax.all_to_all(copies, "col", 0, 0).reshape(cols * local, rows)
    (product,) = local_kernel(product_kernel, [(block, F32)], filtered, diag_blocks)
    peers = ALONG_Y * CORES
    (tiles,) = local_kernel(
        terms_kernel, [((peers, 8, 128), F32)], filtered, product, arrived, all_states
    )
    parts = lax.all_to_all(tiles, ("y", "core"), 0, 0)
    (copies,) = local_kernel(sum_kernel, [((ALONG_X, 8, 128), F32)], parts)
    parts = lax.all_to_all(copies, "x", 0, 0)
    (copies,) = local_kernel(sum_kernel, [((ALONG_Y * cols, 8, 128), F32)], parts)
    shares = lax.all_to_all(copies, ("y", "col"), 0, 0)
    sums = lax.all_gather(shares, "core").reshape(CORES, ALONG_Y, cols, 8, 128)
    return finish(col, sums, all_states, local)


def solution(mesh):
    shape = (ALONG_X, ALONG_Y, CORES, mesh.shape["col"])
    fine = Mesh(mesh.devices.reshape(shape), DOM + ("col",))
    placed = (P("col", DOM), P(DOM, None), P(DOM, None), P(DOM))
    return jax.shard_map(
        body, mesh=fine, in_specs=placed, out_specs=(P("col", DOM), P()), check_vma=False
    )
```

```python
import math

import jax
import jax.numpy as jnp
from jax import lax
from jax.experimental import pallas as pl
from jax.experimental.pallas import tpu as pltpu
from jax.sharding import Mesh
from jax.sharding import PartitionSpec as P

DEGREE = 3
HIGH = lax.Precision.HIGHEST
CENTER = 0.5
HALF = 2.0
PLAIN = (((1,), (0,)), ((), ()))
TRANSPOSED = (((1,), (1,)), ((), ()))
FIRST_WITH_FIRST = (((0,), (0,)), ((), ()))
ALONG_X, ALONG_Y, CORES = 8, 8, 2
DOM = ("x", "y", "core")
WIDE = 64
EVALUATIONS = 3
CLOSE = 1.6e-5
F32 = jnp.float32
BF16 = jnp.bfloat16


def factor_rows(block, wide):
    done = []
    rest = block
    for start in range(0, wide, 8):
        cols = [
            jnp.broadcast_to(rest[:, start + q : start + q + 1], rest.shape) for q in range(8)
        ]
        rows = [rest[q : q + 1, :] for q in range(8)]
        scaled = []
        for p in range(8):
            pivot = cols[p][p : p + 1, :]
            inv = 1.0 / pivot
            scaled.append(rows[p] * inv)
            for q in range(p + 1, 8):
                link = cols[p][q : q + 1, :]
                rows[q] = rows[q] - link * scaled[p]
                cols[q] = cols[q] - cols[p] * (link * inv)
            done.append(rows[p] * lax.rsqrt(pivot))
        if start + 8 < wide:
            change = cols[0][8:, :] * scaled[0]
            for p in range(1, 8):
                change = change + cols[p][8:, :] * scaled[p]
            rest = rest[8:, :] - change
    return jnp.concatenate(done, axis=0)


def cholesky_inverse(a_ref, x_ref, inv_ref):
    n, w = a_ref.shape[0], WIDE
    i = lax.broadcasted_iota(jnp.int32, (n, n), 0)
    j = lax.broadcasted_iota(jnp.int32, (n, n), 1)
    x_ref[...] = (i == j).astype(F32)
    eye = x_ref[:w, :w]
    for s in range(0, n, w):
        here = slice(s, s + w)
        block = factor_rows(jnp.concatenate([a_ref[here, here], eye], axis=1), w)
        both = jnp.concatenate([a_ref[here, :], x_ref[here, :]], axis=1)
        out = jnp.dot(block[:, w:], both, precision=HIGH, preferred_element_type=F32)
        inv_ref[here, :] = out[:, n:]
        if s + w < n:
            change = lax.dot_general(
                out[:, s + w : n], out, FIRST_WITH_FIRST, precision=HIGH, preferred_element_type=F32
            )
            a_ref[s + w :, :] = a_ref[s + w :, :] - change[:, :n]
            x_ref[s + w :, :] = x_ref[s + w :, :] - change[:, n:]


def halves(array):
    high = array.astype(BF16)
    return high, (array - high.astype(F32)).astype(BF16)


def product(left, right, dims):
    return lax.dot_general(left, right, dims, preferred_element_type=F32)


def product_of_halves(left, right, dims):
    small = product(left[0], right[1], dims) + product(left[1], right[0], dims)
    return product(left[0], right[0], dims) + small


def newton_inverse(gram, inv_ref):
    n = gram.shape[0]
    i = lax.broadcasted_iota(jnp.int32, (n, n), 0)
    j = lax.broadcasted_iota(jnp.int32, (n, n), 1)
    diagonal = jnp.where(i == j, gram, 0.0)
    down = lax.rsqrt(jnp.sum(diagonal, axis=1, keepdims=True))
    along = lax.rsqrt(jnp.sum(diagonal, axis=0, keepdims=True))
    ident = jnp.where(i == j, 1.0, 0.0)
    weight = jnp.where(i > j, 1.0, 0.5 * ident)
    scaled = jnp.where(i == j, 1.0, gram * down * along)
    parts = halves(scaled)
    x = jnp.where(i > j, -scaled, ident)
    for step in range(EVALUATIONS):
        xs = halves(x)
        if step == 0:
            moved = product(xs[0], parts[0], PLAIN).astype(BF16)
            error = product(moved, xs[0], TRANSPOSED) - ident
        else:
            moved = halves(product_of_halves(xs, parts, PLAIN))
            error = product_of_halves(moved, xs, TRANSPOSED) - ident
        x = x - product((error * weight).astype(BF16), xs[0], PLAIN)
    inv_ref[...] = x * along
    return jnp.sum(error * error)


def finish_kernel(
    col_ref, sums_ref, all_ref, basis_ref, reduced_ref,
    a_ref, q_ref, x_ref, inv_ref, proj_high_ref, proj_low_ref,
):
    cores, along, cols, eight, lanes = sums_ref.shape
    local = basis_ref.shape[0]
    tiles = cores * along
    per_matrix = tiles // 2
    across = a_ref.shape[1] // lanes
    for t in range(tiles):
        target = a_ref if t < per_matrix else q_ref
        block, half = divmod(t % per_matrix, across)
        for z in range(cols):
            top = z * local + block * eight
            target[top : top + eight, half * lanes : (half + 1) * lanes] = sums_ref[t % cores, t // cores, z]
    proj = q_ref[...]
    proj_high_ref[...], proj_low_ref[...] = halves(0.5 * (proj + proj.T))

    def outputs():
        proj = proj_high_ref[...], proj_low_ref[...]
        inverse = halves(inv_ref[...])
        left = product_of_halves(inverse, proj, PLAIN)
        reduced_ref[...] = product_of_halves(halves(left), inverse, TRANSPOSED)
        scale = math.sqrt(ALONG_X * ALONG_Y * CORES * basis_ref.shape[1])
        mine = scale * inv_ref[pl.ds(pl.multiple_of(col_ref[0] * local, local), local), :]
        high, low = halves(mine)
        states = all_ref[...]
        basis_ref[...] = product(high, states, PLAIN) + product(low, states, PLAIN)

    residual = newton_inverse(a_ref[...], inv_ref)
    outputs()

    @pl.when(jnp.logical_not(residual < CLOSE))
    def _():
        cholesky_inverse(a_ref, x_ref, inv_ref)
        outputs()


def finish(col, sums, all_states, local):
    total, rows = all_states.shape
    vmem = pl.BlockSpec(memory_space=pltpu.VMEM)
    square = pltpu.VMEM((total, total), F32)
    return pl.pallas_call(
        finish_kernel,
        out_shape=(
            jax.ShapeDtypeStruct((local, rows), F32),
            jax.ShapeDtypeStruct((total, total), F32),
        ),
        in_specs=[pl.BlockSpec(memory_space=pltpu.SMEM), vmem, vmem],
        out_specs=(vmem, vmem),
        scratch_shapes=[square] * 4 + [pltpu.VMEM((total, total), BF16)] * 2,
        compiler_params=pltpu.CompilerParams(vmem_limit_bytes=32 * 2**20),
        cost_estimate=pl.CostEstimate(flops=2 * 10**8, bytes_accessed=2**21, transcendentals=0),
    )(col, sums, all_states)


def across_pairs(count):
    pairs = [(i, i + 1 if i % 2 else i - 1) for i in range(count)]
    return [(i, j) for i, j in pairs if 0 <= j < count]


def local_kernel(kernel, outs, *operands, scalars=0):
    vmem = pl.BlockSpec(memory_space=pltpu.VMEM)
    smem = pl.BlockSpec(memory_space=pltpu.SMEM)
    return pl.pallas_call(
        kernel,
        out_shape=tuple(jax.ShapeDtypeStruct(shape, dtype) for shape, dtype in outs),
        in_specs=[smem] * scalars + [vmem] * (len(operands) - scalars),
        out_specs=(vmem,) * len(outs),
        compiler_params=pltpu.CompilerParams(vmem_limit_bytes=12 * 2**20),
        cost_estimate=pl.CostEstimate(flops=2**16, bytes_accessed=2**16, transcendentals=0),
    )(*operands)


def own_kernel(low_ref, diag_ref, own_ref):
    low, diag = low_ref[...], diag_ref[...]
    own = jnp.dot(low, diag, preferred_element_type=F32)
    own_t = lax.dot_general(low, diag, TRANSPOSED, preferred_element_type=F32)
    own_ref[...] = 0.5 * (own + own_t)


def copies_kernel(array_ref, copies_hbm, sems):
    copies = [
        pltpu.make_async_copy(array_ref, copies_hbm.at[i], sems.at[i])
        for i in range(copies_hbm.shape[0])
    ]
    for copy in copies:
        copy.start()
    for copy in copies:
        copy.wait()


def copied(array, count):
    return pl.pallas_call(
        copies_kernel,
        out_shape=jax.ShapeDtypeStruct((count,) + array.shape, array.dtype),
        in_specs=[pl.BlockSpec(memory_space=pltpu.VMEM)],
        out_specs=pl.BlockSpec(memory_space=pltpu.HBM),
        scratch_shapes=[pltpu.SemaphoreType.DMA((count,))],
        compiler_params=pltpu.CompilerParams(vmem_limit_bytes=12 * 2**20),
        cost_estimate=pl.CostEstimate(flops=0, bytes_accessed=2**16, transcendentals=0),
    )(array)


def product_kernel(left_ref, right_ref, out_ref):
    out = jnp.dot(left_ref[...], right_ref[...], preferred_element_type=F32)
    out_ref[...] = out.astype(out_ref.dtype)


def terms_kernel(filtered_ref, product_ref, arrived_ref, all_ref, tiles_ref):
    half_image = (product_ref[...] + 2.0 * arrived_ref[...].astype(F32)).astype(BF16)
    pair = jnp.concatenate([filtered_ref[...], half_image], axis=0)
    terms = lax.dot_general(pair, all_ref[...], TRANSPOSED, preferred_element_type=F32)
    across = terms.shape[1] // 128
    for t in range(tiles_ref.shape[0]):
        k, half = divmod(t, across)
        tiles_ref[t] = terms[8 * k : 8 * k + 8, 128 * half : 128 * half + 128]


def sum_kernel(parts_ref, copies_ref):
    total = parts_ref[0]
    for i in range(1, parts_ref.shape[0]):
        total = total + parts_ref[i]
    for i in range(copies_ref.shape[0]):
        copies_ref[i] = total


def body(states, diag_blocks, coupling, counts):
    local, rows = states.shape
    block = (local, rows)
    domains, cols = lax.axis_size(DOM), lax.axis_size("col")
    core = lax.axis_index("core").astype(jnp.int32).reshape(1)
    col = lax.axis_index("col").astype(jnp.int32).reshape(1)

    live = (lax.iota(jnp.int32, rows) < counts[0])[None, :]
    low = lax.optimization_barrier(jnp.where(live, states, jnp.zeros_like(states)))
    even = core[0] == 0
    history = [low.astype(F32)]
    for step in range(DEGREE):
        onward = jnp.dot(low, coupling, preferred_element_type=F32)
        over = jnp.where(even, history[-1], onward)
        on = jnp.where(even, onward, history[-1])
        over = lax.ppermute(over, DOM, across_pairs(domains))
        both = lax.all_gather(on, "core")
        low, both, col = lax.optimization_barrier((low, both, col))
        (own,) = local_kernel(own_kernel, [(block, F32)], low, diag_blocks)
        beside = jnp.where(even, both[1], both[0])
        next_block = jnp.where(even, beside, over).astype(BF16)
        from_next = lax.dot_general(
            next_block, coupling, TRANSPOSED, preferred_element_type=F32
        )
        image = jnp.where(live, own + jnp.where(even, over, beside) + from_next, 0.0)
        cur = (image - CENTER * history[-1]) / HALF
        if step > 0:
            cur = 2.0 * cur - history[-2]
        history.append(cur)
        low = cur.astype(BF16)
    filtered = lax.optimization_barrier(low)
    copies = copied(filtered, cols)

    onward = jnp.dot(filtered, coupling, preferred_element_type=F32).astype(BF16)
    arrived = lax.ppermute(onward, DOM, [(i, i + 1) for i in range(domains - 1)])
    all_states = lax.all_to_all(copies, "col", 0, 0).reshape(cols * local, rows)
    (product,) = local_kernel(product_kernel, [(block, F32)], filtered, diag_blocks)
    peers = ALONG_Y * CORES
    (tiles,) = local_kernel(
        terms_kernel, [((peers, 8, 128), F32)], filtered, product, arrived, all_states
    )
    parts = lax.all_to_all(tiles, ("y", "core"), 0, 0)
    (copies,) = local_kernel(sum_kernel, [((ALONG_X, 8, 128), F32)], parts)
    parts = lax.all_to_all(copies, "x", 0, 0)
    (copies,) = local_kernel(sum_kernel, [((ALONG_Y * cols, 8, 128), F32)], parts)
    shares = lax.all_to_all(copies, ("y", "col"), 0, 0)
    sums = lax.all_gather(shares, "core").reshape(CORES, ALONG_Y, cols, 8, 128)
    return finish(col, sums, all_states, local)


def solution(mesh):
    shape = (ALONG_X, ALONG_Y, CORES, mesh.shape["col"])
    fine = Mesh(mesh.devices.reshape(shape), DOM + ("col",))
    placed = (P("col", DOM), P(DOM, None), P(DOM, None), P(DOM))
    return jax.shard_map(
        body, mesh=fine, in_specs=placed, out_specs=(P("col", DOM), P()), check_vma=False
    )
```
